128 devices in a mesh: rep: 8 (over x, z_lo), tp: 16 (over z_hi, y, core).
Axes of the slice: x: 4, y: 4, z: 4 (z_hi: 2, z_lo: 2; z = z_hi * 2 + z_lo), core: 2. Of those that a mesh axis runs over, the one named last changes fastest.
Arguments:
- pool_tokens: bfloat16 [1024, 4096], P('tp'), may hold values from -6 to 6
- pool_targets: bfloat16 [1024, 4096], P('tp'), may hold values from -6 to 6
- pick: int32 [8, 2, 384], P('rep', None, 'tp'), may hold values from 0 to 63
- up_weight: bfloat16 [4096, 14336], P(None, 'tp'), may hold values from -6 to 6
- down_weight: bfloat16 [14336, 4096], P('tp'), may hold values from -6 to 6
Outputs:
- new_down: bfloat16 [14336, 4096], P('tp')
The draws below stay inside these ranges and needn't reach their ends.
Inputs may be any that keep to these rules, and one draw needn't show every extreme that they name: pick[r, s, t] counts from the first of the 64 pool rows held on the same tp index as token t.
All inputs are finite; a program needn't handle non-finite values.
Results may differ from the reference program's by a relative error of at most 0.011.
Values may be sent and summed in bfloat16 or wider, within the bound.
A program may use at most 128 MiB of HBM per device.

```python
import jax
import jax.numpy as jnp

D = 4096
TOK_DEV = 24
POOL_DEV = 64
STEPS = 2
FF = 14336
TOKENS = 384
POOL = 1024
REPLICAS = 8


def plant(array, rng, least, largest):
    dims = array.shape
    place = [jax.random.randint(jax.random.fold_in(rng, axis), (), 0, dims[axis]) for axis in range(len(dims))]
    array = array.at[tuple(place)].set(least)
    longest = dims.index(max(dims))
    place[longest] = (place[longest] + 1) % dims[longest]
    return array.at[tuple(place)].set(largest)


def block_scale(key, dims, shards, low, largest):
    def one(position, shards_of):
        draws = jax.random.uniform(jax.random.fold_in(jax.random.fold_in(key, 6), position), (shards_of,), jnp.float32, low / len(shards), largest / len(shards))
        return jnp.repeat(jnp.exp(draws), dims[position] // shards_of).reshape((-1,) + (1,) * (len(dims) - position - 1))

    loudness = one(*shards[0])
    for cut in shards[1:]:
        loudness = loudness * one(*cut)
    return loudness


def normal_values(rng, dims, deviation, bound, shards=(), held_as=jnp.bfloat16):
    loudness = block_scale(rng, dims, shards, -0.22, 0.18) if shards else 1.0
    values = jax.random.normal(rng, dims, jnp.float32) * deviation * loudness
    return jnp.minimum(jnp.maximum(values, -bound), bound).astype(held_as)


def setup_inputs(seed: int = 0) -> dict:
    streams_of = jax.random.split(jax.random.key(seed), 6)
    return {
        "pool_tokens": normal_values(streams_of[0], (POOL, D), 1.0, 6.0, ((0, 16),)),
        "pool_targets": normal_values(streams_of[1], (POOL, D), 1.0, 6.0, ((0, 16),)),
        "pick": plant(jax.random.randint(streams_of[2], (REPLICAS, STEPS, TOKENS), 0, POOL_DEV), jax.random.fold_in(streams_of[2], 1), 0, POOL_DEV - 1).astype(jnp.int32),
        "up_weight": normal_values(streams_of[3], (D, FF), 1.0, 6.0, ((1, 16),)),
        "down_weight": normal_values(streams_of[4], (FF, D), 1.0, 6.0, ((0, 16),)),
    }


def silu_slope(preact):
    sigma = jax.nn.sigmoid(preact)
    return sigma * (1.0 + preact * (1.0 - sigma))

def adamw(weight, grad, first, second, count):
    first = 0.9 * first + 0.1 * grad
    second = 0.95 * second + 0.05 * grad * grad
    first_hat = first / (1.0 - 0.9 ** count)
    second_hat = second / (1.0 - 0.95 ** count)
    weight = weight - 0.25 * (first_hat / (jnp.sqrt(second_hat) + 0.02) + 0.1 * weight)
    return (weight, first, second)

def forward(inputs, goals, up_cast, down_cast):
    scale_up = D ** (-0.5)
    scale_down = FF ** (-0.5)
    preact = scale_up * jnp.dot(inputs, up_cast, preferred_element_type=jnp.float32)
    hidden = jax.nn.silu(preact).astype(jnp.bfloat16)
    output = inputs.astype(jnp.float32) + scale_down * jnp.dot(hidden, down_cast, preferred_element_type=jnp.float32)
    error = (output - goals.astype(jnp.float32)).astype(jnp.bfloat16)
    grad_down = scale_down * jnp.dot(hidden.T, error, preferred_element_type=jnp.float32)
    return (preact, error, grad_down)

def replica_delta(pool_tokens, pool_targets, chosen, up_weight, down_weight):
    owner = jnp.arange(TOKENS, dtype=jnp.int32) // TOK_DEV
    first_rows = owner * POOL_DEV + chosen[0].astype(jnp.int32)
    second_rows = owner * POOL_DEV + chosen[1].astype(jnp.int32)
    up_master = up_weight.astype(jnp.float32)
    down_start = down_weight.astype(jnp.float32)
    inputs = pool_tokens[first_rows]
    goals = pool_targets[first_rows]
    preact, error, grad_down = forward(inputs, goals, up_weight, down_weight)
    slope_pre = FF ** (-0.5) * jnp.dot(error, down_weight.T, preferred_element_type=jnp.float32)
    slope = (slope_pre * silu_slope(preact)).astype(jnp.bfloat16)
    grad_up = D ** (-0.5) * jnp.dot(inputs.T, slope, preferred_element_type=jnp.float32)
    zeros_up = jnp.zeros(up_master.shape, jnp.float32)
    zeros_down = jnp.zeros(down_start.shape, jnp.float32)
    up_master, first_up, second_up = adamw(up_master, grad_up, zeros_up, zeros_up, 1)
    down_master, first_down, second_down = adamw(down_start, grad_down, zeros_down, zeros_down, 1)
    inputs = pool_tokens[second_rows]
    goals = pool_targets[second_rows]
    preact, error, grad_down = forward(inputs, goals, up_master.astype(jnp.bfloat16), down_master.astype(jnp.bfloat16))
    down_master, first_down, second_down = adamw(down_master, grad_down, first_down, second_down, 2)
    return down_start - down_master

def reference(pool_tokens, pool_targets, pick, up_weight, down_weight):
    total = jnp.zeros((FF, D), jnp.float32)
    for replica in range(REPLICAS):
        total = total + replica_delta(pool_tokens, pool_targets, pick[replica], up_weight, down_weight)
    average = total / REPLICAS
    momentum = average
    new_down = down_weight.astype(jnp.float32) - 0.7 * (average + 0.9 * momentum)
    return new_down.astype(jnp.bfloat16)
```

```python
import functools
import math

import jax
import jax.numpy as jnp
from jax import lax
from jax.experimental import pallas as pl
from jax.experimental.pallas import tpu as pltpu
from jax.sharding import PartitionSpec as P

MESH = pl.DeviceIdType.MESH
BF, F32 = jnp.bfloat16, jnp.float32

CORE = (0, 0, 0, 0, 1)
YP, YM = (0, 0, 0, 1, 0), (0, 0, 0, -1, 0)
ZH = (0, 0, 1, 0, 0)
XP, XM, X2, ZL = (1, 0, 0, 0, 0), (-1, 0, 0, 0, 0), (2, 0, 0, 0, 0), (0, 1, 0, 0, 0)
REP = (None, XP, XM, X2, ZL, (1, 1, 0, 0, 0), (-1, 1, 0, 0, 0), (2, 1, 0, 0, 0))

TOK = 48
HALF = 2048
ROWS = 384
SLICE = 256
CHUNKS = 4


def place():
    r, t = lax.axis_index("rep"), lax.axis_index("tp")
    return r // 2, r % 2, t // 8, (t // 2) % 4, t % 2


def rep_index(off):
    x, zl, _, _, _ = place()
    return ((x + off[0] + 4) % 4) * 2 + (zl + off[1]) % 2


def target(off):
    _, _, zh, y, core = place()
    tp = (((zh + off[2]) % 2) * 4 + (y + off[3] + 4) % 4) * 2 + (core + off[4]) % 2
    return (rep_index(off), tp)


class Sends:
    def __init__(self, send_sems, recv_sems):
        self.send_sems, self.recv_sems, self.count = send_sems, recv_sems, 0

    def __call__(self, src, dst, off):
        k = self.count
        self.count += 1
        copy = pltpu.make_async_remote_copy(
            src_ref=src,
            dst_ref=dst,
            send_sem=self.send_sems.at[k],
            recv_sem=self.recv_sems.at[k],
            device_id=target(off),
            device_id_type=MESH,
        )
        copy.start()
        return copy


class GatherTp:
    def __init__(self, send, buf, rows, part):
        self.send, self.buf, self.rows, self.part = send, buf, rows, part
        self.core = place()[4]
        self.done = []
        self.sib = []

    def slot(self, k):
        return self.buf.at[self.core, pl.ds(k * self.rows, self.rows)]

    def go(self, src, dst, h, off):
        copy = self.send(self.part(self.slot(src), h), self.part(self.slot(dst), h), off)
        self.done.append(copy)
        return copy

    def sibling(self, k):
        self.sib.append(self.send(self.slot(k), self.slot(k), CORE))

    def p1(self):
        self.z = [self.go(0, 4, 0, ZH), self.go(0, 4, 1, ZH)]
        self.p0 = self.go(0, 1, 0, YP)
        self.m1 = self.go(0, 2, 1, YM)
        self.p1_ = self.go(0, 1, 1, YP)
        self.m0 = self.go(0, 2, 0, YM)
        self.sibling(0)

    def p2(self):
        self.z[0].wait_recv()
        self.q0 = self.go(4, 5, 0, YP)
        self.z[1].wait_recv()
        self.n1 = self.go(4, 6, 1, YM)
        self.q1 = self.go(4, 5, 1, YP)
        self.n0 = self.go(4, 6, 0, YM)
        self.sibling(4)

    def p3(self):
        self.p0.wait_recv()
        self.f1 = self.go(1, 3, 0, YP)
        self.m1.wait_recv()
        self.f2 = self.go(2, 3, 1, YM)
        self.p1_.wait_recv()
        self.sibling(1)
        self.m0.wait_recv()
        self.sibling(2)
        self.q0.wait_recv()
        self.f3 = self.go(5, 7, 0, YP)
        self.n1.wait_recv()
        self.f4 = self.go(6, 7, 1, YM)

    def p4(self):
        self.f1.wait_recv()
        self.f2.wait_recv()
        self.sibling(3)
        self.q1.wait_recv()
        self.sibling(5)
        self.n0.wait_recv()
        self.sibling(6)
        self.f3.wait_recv()
        self.f4.wait_recv()
        self.sibling(7)

    def p5(self):
        for copy in self.sib:
            copy.wait_recv()
        for copy in self.sib + self.done:
            copy.wait_send()

    def all(self):
        self.p1()
        self.p2()
        self.p3()
        self.p4()
        self.p5()


class GatherRep:
    def __init__(self, send, ref):
        self.send, self.ref = send, ref
        self.first, self.second, self.third = {}, {}, {}

    def go(self, src, dst, j, off):
        return [self.send(a, b, off) for a, b in zip(self.ref(src, j), self.ref(dst, j, off))]

    def a(self, j):
        self.first[j] = (self.go(0, 4, j, ZL), self.go(0, 1, j, XP), self.go(0, 2, j, XM))

    def b(self, j):
        for copies in self.first[j]:
            for copy in copies:
                copy.wait_recv()
        f = self.go(1, 3, j, XP) if j % 2 == 0 else self.go(2, 3, j, XM)
        if (j // 2) % 2 == 0:
            more = (self.go(4, 5, j, XP), self.go(4, 6, j, XM))
        else:
            more = (self.go(1, 5, j, ZL), self.go(2, 6, j, ZL))
        self.second[j] = (f,) + more

    def c(self, j):
        for copies in self.second[j]:
            for copy in copies:
                copy.wait_recv()
        if (j // 2) % 2 == 0:
            self.third[j] = self.go(5, 7, j, XP) if j % 2 == 1 else self.go(6, 7, j, XM)
        else:
            self.third[j] = self.go(3, 7, j, ZL)

    def end(self, j):
        for copy in self.third[j]:
            copy.wait_recv()
        for copies in self.first[j] + self.second[j] + (self.third[j],):
            for copy in copies:
                copy.wait_send()


def columns_part(ref, h):
    return ref.at[:, pl.ds(h * (HALF // 2), HALF // 2)]


def rows_part(ref, h):
    return ref.at[pl.ds(h * (ROWS // 2), ROWS // 2)]


def body(
    scale_up,
    scale_down,
    mine,
    other,
    up_hbm,
    down_hbm,
    out,
    up,
    down,
    down_own,
    sib_prep,
    local,
    tok0,
    tok1,
    pre,
    hid,
    ht0,
    ht1,
    sib_send,
    sib_recv,
    part,
    r_far,
    r_near,
    r_z,
    err0,
    es0,
    es1,
    res,
    send_sems,
    recv_sems,
    copy_sems,
):
    _, _, _, _, core = place()
    me = lax.axis_index("rep")
    send = Sends(send_sems, recv_sems)

    loads = [
        pltpu.make_async_copy(up_hbm, up, copy_sems.at[0]),
        pltpu.make_async_copy(down_hbm, down, copy_sems.at[1]),
    ]
    for h in range(2):
        cols = pl.ds(pl.multiple_of(h * HALF + me * SLICE, SLICE), SLICE)
        loads.append(pltpu.make_async_copy(down_hbm.at[:, cols], down_own.at[h], copy_sems.at[2 + h]))
    for load in loads:
        load.start()

    peers = (CORE, YP, YM, ZH) + REP[1:]
    barrier = pltpu.get_barrier_semaphore()
    for off in peers:
        pl.semaphore_signal(barrier, inc=1, device_id=target(off), device_id_type=MESH)
    pl.semaphore_wait(barrier, len(peers))

    prep = send(other, sib_prep, CORE)
    prep.wait_recv()
    for i in range(4):
        rows = pl.ds(24 * i, 24)
        a, b = mine[rows, :].astype(F32), sib_prep[rows, :].astype(F32)
        first, second = jnp.where(core == 0, a, b), jnp.where(core == 0, b, a)
        local[i] = jnp.concatenate([first, second], axis=0).astype(BF)
    prep.wait_send()
    tok0[core, pl.ds(0, TOK), :] = local[0]
    tok1[core, pl.ds(0, TOK), :] = local[2]

    def preact(tokens):
        pre[...] = jnp.zeros_like(pre)
        for h in range(2):

            @pl.loop(0, HALF // 512)
            def _(k):
                cols = pl.ds(pl.multiple_of(k * 512, 512), 512)
                rows = pl.ds(pl.multiple_of(h * HALF + k * 512, 512), 512)
                pre[...] += jnp.dot(tokens[h, :, cols], up[rows, :], preferred_element_type=F32)

    def activate(ht):
        @pl.loop(0, 7)
        def _(k):
            cols = pl.ds(pl.multiple_of(k * 128, 128), 128)
            v = pre[:, cols] * scale_up
            hidden = (v * jax.nn.sigmoid(v)).astype(BF)
            hid[:, cols] = hidden
            ht[0, cols, :] = hidden.T

    def layer_out(base, width, store):
        @pl.loop(0, width // 512)
        def _(k):
            inner = pl.multiple_of(k * 512, 512)
            cols = pl.ds(pl.multiple_of(base + inner, 512), 512)
            store(inner, jnp.dot(hid[...], down[:, cols], preferred_element_type=F32))

    def forward_down(between):
        sib = []
        for h in range(2):

            def to_sibling(inner, value, h=h):
                sib_send[h, :, pl.ds(inner, 512)] = value.astype(BF)

            layer_out((1 - core) * HALF + h * 1024, 1024, to_sibling)
            sib.append(send(sib_send.at[h], sib_recv.at[h], CORE))
        between()
        for h in range(2):
            sib[h].wait_recv()

            def to_part(inner, value, h=h):
                total = value + sib_recv[h, :, pl.ds(inner, 512)].astype(F32)
                part[h, :, pl.ds(inner, 512)] = total.astype(BF)

            layer_out(core * HALF + h * 1024, 1024, to_part)
        for copy in sib:
            copy.wait_send()

    def scatter():
        sent = []

        def go(src, dst, off):
            copy = send(src, dst, off)
            sent.append(copy)
            return copy

        def block(k, h):
            return part.at[h, pl.ds(k * TOK, TOK)]

        far, near = {}, {}
        for p in (1, 0):
            far[p, 0] = go(block(4 * p + 3, 0), r_far.at[p, 0], YP)
            far[p, 1] = go(block(4 * p + 3, 1), r_far.at[p, 1], YM)
            near[p, 0, 1] = go(block(4 * p + 2, 1), r_near.at[p, 0, 1], YP)
            near[p, 1, 0] = go(block(4 * p + 1, 0), r_near.at[p, 1, 0], YM)
        for p in (1, 0):
            for d, off in ((0, YP), (1, YM)):
                far[p, d].wait_recv()
                rows = pl.ds((4 * p + 2 - d) * TOK, TOK)
                total = part[d, rows, :].astype(F32) + r_far[p, d].astype(F32)
                part[d, rows, :] = total.astype(BF)
                near[p, d, d] = go(block(4 * p + 2 - d, d), r_near.at[p, d, d], off)
        z = []
        for h in range(2):
            near[1, 0, h].wait_recv()
            near[1, 1, h].wait_recv()
            rows = pl.ds(4 * TOK, TOK)
            total = part[h, rows, :].astype(F32) + r_near[1, 0, h].astype(F32) + r_near[1, 1, h].astype(F32)
            part[h, rows, :] = total.astype(BF)
            z.append(go(block(4, h), r_z.at[h], ZH))
        halves = []
        for h in range(2):
            near[0, 0, h].wait_recv()
            near[0, 1, h].wait_recv()
            total = part[h, pl.ds(0, TOK), :].astype(F32) + r_near[0, 0, h].astype(F32) + r_near[0, 1, h].astype(F32)
            z[h].wait_recv()
            halves.append(total + r_z[h].astype(F32))
        for copy in sent:
            copy.wait_send()
        return halves

    def error(step, halves, dst, es):
        for h in range(2):
            cols = pl.ds(h * 1024, 1024)
            value = local[2 * step, :, cols].astype(F32) + scale_down * halves[h] - local[2 * step + 1, :, cols].astype(F32)
            dst[:, cols] = value.astype(BF)
        sent = []
        for k in range(1, 8):
            cols = pl.ds(pl.multiple_of(rep_index(REP[k]) * SLICE, SLICE), SLICE)
            sent.append(send(dst.at[:, cols], es.at[core, pl.ds(k * TOK, TOK)], REP[k]))
        cols = pl.ds(pl.multiple_of(me * SLICE, SLICE), SLICE)
        es[core, pl.ds(0, TOK), :] = dst[:, cols]
        return sent

    def hidden_gather(ht):
        size = ht.shape[1] // CHUNKS
        return GatherRep(send, lambda slot, j, off=None: [ht.at[slot, pl.ds(j * size, size)]])

    GatherTp(send, tok0, TOK, columns_part).all()
    late = GatherTp(send, tok1, TOK, columns_part)
    late.p1()
    loads[0].wait()
    preact(tok0)
    late.p2()
    activate(ht0)
    rep0 = hidden_gather(ht0)
    for j in range(CHUNKS):
        rep0.a(j)
    loads[1].wait()
    forward_down(late.p3)
    halves = scatter()
    late.p4()
    sliced = error(0, halves, err0.at[core, pl.ds(0, TOK)], es0)
    gather = GatherTp(send, err0, TOK, columns_part)
    gather.p1()
    for j in range(CHUNKS):
        rep0.b(j)
    gather.p2()
    gather.p3()
    gather.p4()
    gather.p5()
    for copy in sliced:
        copy.wait()
    slices = GatherTp(send, es0, ROWS, rows_part)
    slices.p1()

    @pl.loop(0, 3)
    def _(n):
        rows = pl.ds(pl.multiple_of(n * 128, 128), 128)
        total = jnp.zeros((128, 896), F32)
        for h in range(2):
            for k in range(2):
                cols = pl.ds(k * 1024, 1024)
                total += lax.dot_general(
                    err0[h, rows, cols],
                    down[:, pl.ds(h * HALF + k * 1024, 1024)],
                    (((1,), (1,)), ((), ())),
                    preferred_element_type=F32,
                )
        v = pre[rows, :] * scale_up
        sigma = jax.nn.sigmoid(v)
        hid[rows, :] = (scale_down * total * (sigma * (1.0 + v * (1.0 - sigma)))).astype(BF)

    slices.p2()
    for h in range(2):

        @pl.loop(0, HALF // 256)
        def _(k):
            cols = pl.ds(pl.multiple_of(k * 256, 256), 256)
            rows = pl.ds(pl.multiple_of(h * HALF + k * 256, 256), 256)
            g = jnp.dot(tok0[h, :, cols].T, hid[...], preferred_element_type=F32)
            u = g / (jnp.abs(g) + 0.02 / scale_up)
            up[rows, :] = (0.975 * up[rows, :].astype(F32) - 0.25 * u).astype(BF)

    slices.p3()
    for j in range(CHUNKS):
        rep0.c(j)
    late.p5()
    for h in range(2):

        @pl.loop(0, HALF // 256)
        def _(k):
            cols = pl.ds(pl.multiple_of(k * 256, 256), 256)
            wide = pl.ds(pl.multiple_of(h * HALF + k * 256, 256), 256)
            g = jnp.dot(ht0[0], err0[h, :, cols], preferred_element_type=F32)
            u = g / (jnp.abs(g) + 0.02 / scale_down)
            down[:, wide] = (0.975 * down[:, wide].astype(F32) - 0.25 * u).astype(BF)

    slices.p4()
    for j in range(CHUNKS):
        rep0.end(j)

    preact(tok1)
    activate(ht1)
    rep1 = hidden_gather(ht1)
    for j in range(CHUNKS):
        rep1.a(j)
    forward_down(slices.p5)
    halves = scatter()
    sliced = error(1, halves, local.at[0], es1)
    for j in range(CHUNKS):
        rep1.b(j)
    for copy in sliced:
        copy.wait()
    last = GatherTp(send, es1, ROWS, rows_part)
    last.p1()
    last.p2()
    last.p3()
    for j in range(CHUNKS):
        rep1.c(j)
    last.p4()
    last.p5()
    for j in range(CHUNKS):
        rep1.end(j)
    loads[2].wait()
    loads[3].wait()

    size = 896 // CHUNKS

    def reduce(j, h):
        rows = pl.ds(j * size, size)

        def one(k, total):
            tokens = pl.ds(pl.multiple_of(k * TOK, TOK), TOK)
            e0 = es0_view[h, :, tokens, :].reshape(ROWS, SLICE)
            e1 = es1_view[h, :, tokens, :].reshape(ROWS, SLICE)
            g0 = jnp.dot(ht0[k, rows, :], e0, preferred_element_type=F32)
            g1 = jnp.dot(ht1[k, rows, :], e1, preferred_element_type=F32)
            u0 = g0 / (jnp.abs(g0) + 0.02 / scale_down)
            first = (0.09 / 0.19) * g0 + (0.1 / 0.19) * g1
            second = (0.0475 / 0.0975) * (g0 * g0) + (0.05 / 0.0975) * (g1 * g1)
            u1 = first / (jnp.sqrt(second) + 0.02 / scale_down)
            return total + (0.975 * u0 + u1)

        total = lax.fori_loop(0, 8, one, jnp.zeros((size, SLICE), F32))
        w = down_own[h, rows, :].astype(F32)
        average = (1.0 - 0.975 * 0.975) * w + (0.25 / 8.0) * total
        res[h, rows, :] = (w - 0.7 * 1.9 * average).astype(BF)

    es0_view = es0.reshape(2, 8, ROWS, SLICE)
    es1_view = es1.reshape(2, 8, ROWS, SLICE)

    def pieces(slot, j, off=None):
        rows = pl.ds(j * size, size)
        if slot == 0:
            return [res.at[h, rows] for h in range(2)]
        back = REP[slot]
        shift = off if off is not None else (0, 0)
        r = rep_index((shift[0] - back[0] + 4, shift[1] - back[1] + 2))
        return [out.at[rows, pl.ds(pl.multiple_of(h * HALF + r * SLICE, SLICE), SLICE)] for h in range(2)]

    final = GatherRep(send, pieces)
    own = []
    for j in range(CHUNKS):
        for h in range(2):
            reduce(j, h)
        final.a(j)
        for h in range(2):
            cols = pl.ds(pl.multiple_of(h * HALF + me * SLICE, SLICE), SLICE)
            rows = pl.ds(j * size, size)
            own.append(pltpu.make_async_copy(res.at[h, rows], out.at[rows, cols], copy_sems.at[4 + 2 * j + h]))
            own[-1].start()
        if j >= 1:
            final.b(j - 1)
        if j >= 2:
            final.c(j - 2)
    final.b(CHUNKS - 1)
    final.c(CHUNKS - 2)
    final.c(CHUNKS - 1)
    for j in range(CHUNKS):
        final.end(j)
    for copy in own:
        copy.wait()


SEMS = 300


def round_kernel(mine, other, up_weight, down_weight, scale_up, scale_down):
    vmem, anywhere = pl.BlockSpec(memory_space=pltpu.VMEM), pl.BlockSpec(memory_space=pl.ANY)
    width, hidden = up_weight.shape
    return pl.pallas_call(
        functools.partial(body, scale_up, scale_down),
        out_shape=jax.ShapeDtypeStruct(down_weight.shape, BF),
        in_specs=[vmem, vmem, anywhere, anywhere],
        out_specs=anywhere,
        scratch_shapes=[
            pltpu.VMEM((width, hidden), BF),
            pltpu.VMEM((hidden, width), BF),
            pltpu.VMEM((2, hidden, SLICE), BF),
            pltpu.VMEM((96, HALF), BF),
            pltpu.VMEM((4, TOK, HALF), BF),
            pltpu.VMEM((2, ROWS, HALF), BF),
            pltpu.VMEM((2, ROWS, HALF), BF),
            pltpu.VMEM((ROWS, hidden), F32),
            pltpu.VMEM((ROWS, hidden), BF),
            pltpu.VMEM((8, hidden, ROWS), BF),
            pltpu.VMEM((8, hidden, ROWS), BF),
            pltpu.VMEM((2, ROWS, HALF // 2), BF),
            pltpu.VMEM((2, ROWS, HALF // 2), BF),
            pltpu.VMEM((2, ROWS, HALF // 2), BF),
            pltpu.VMEM((2, 2, TOK, HALF // 2), BF),
            pltpu.VMEM((2, 2, 2, TOK, HALF // 2), BF),
            pltpu.VMEM((2, TOK, HALF // 2), BF),
            pltpu.VMEM((2, ROWS, HALF), BF),
            pltpu.VMEM((2, 8 * ROWS, SLICE), BF),
            pltpu.VMEM((2, 8 * ROWS, SLICE), BF),
            pltpu.VMEM((2, hidden, SLICE), BF),
            pltpu.SemaphoreType.DMA((SEMS,)),
            pltpu.SemaphoreType.DMA((SEMS,)),
            pltpu.SemaphoreType.DMA((4 + 2 * CHUNKS,)),
        ],
        compiler_params=pltpu.CompilerParams(
            collective_id=0, has_side_effects=True, vmem_limit_bytes=62 * 2**20
        ),
    )(mine, other, up_weight, down_weight)


def per_device(pool_tokens, pool_targets, pick, up_weight, down_weight):
    core = lax.axis_index("tp") % 2
    chosen = pick[0]
    rows = jnp.concatenate(
        [jnp.take(pool, chosen[step], axis=0) for step in range(2) for pool in (pool_tokens, pool_targets)], axis=0
    )
    mine = lax.dynamic_slice_in_dim(rows, core * HALF, HALF, axis=1)
    other = lax.dynamic_slice_in_dim(rows, (1 - core) * HALF, HALF, axis=1)
    scale_up = 1.0 / math.sqrt(up_weight.shape[0])
    scale_down = 1.0 / math.sqrt(up_weight.shape[1] * lax.axis_size("tp"))
    return round_kernel(mine, other, up_weight, down_weight, scale_up, scale_down)


def solution(mesh):
    in_specs = (P("tp", None), P("tp", None), P("rep", None, "tp"), P(None, "tp"), P("tp", None))
    return jax.shard_map(per_device, mesh=mesh, in_specs=in_specs, out_specs=P("tp", None), check_vma=False)
```

```python
import functools
import math

import jax
import jax.numpy as jnp
from jax import lax
from jax.experimental import pallas as pl
from jax.experimental.pallas import tpu as pltpu
from jax.sharding import PartitionSpec as P

MESH = pl.DeviceIdType.MESH
BF, F32 = jnp.bfloat16, jnp.float32

CORE = (0, 0, 0, 0, 1)
YP, YM = (0, 0, 0, 1, 0), (0, 0, 0, -1, 0)
ZH = (0, 0, 1, 0, 0)
XP, XM, X2, ZL = (1, 0, 0, 0, 0), (-1, 0, 0, 0, 0), (2, 0, 0, 0, 0), (0, 1, 0, 0, 0)
REP = (None, XP, XM, X2, ZL, (1, 1, 0, 0, 0), (-1, 1, 0, 0, 0), (2, 1, 0, 0, 0))

TOK = 48
HALF = 2048
ROWS = 384
SLICE = 256
CHUNKS = 4


def place():
    r, t = lax.axis_index("rep"), lax.axis_index("tp")
    return r // 2, r % 2, t // 8, (t // 2) % 4, t % 2


def rep_index(off):
    x, zl, _, _, _ = place()
    return ((x + off[0] + 4) % 4) * 2 + (zl + off[1]) % 2


def target(off):
    _, _, zh, y, core = place()
    tp = (((zh + off[2]) % 2) * 4 + (y + off[3] + 4) % 4) * 2 + (core + off[4]) % 2
    return (rep_index(off), tp)


def inverse(v):
    return pl.reciprocal(v, approx=True)


def run(hook):
    if hook is not None:
        hook()


class Sends:
    def __init__(self, send_sems, recv_sems):
        self.send_sems, self.recv_sems, self.count = send_sems, recv_sems, 0

    def __call__(self, src, dst, off):
        k = self.count
        self.count += 1
        copy = pltpu.make_async_remote_copy(
            src_ref=src,
            dst_ref=dst,
            send_sem=self.send_sems.at[k],
            recv_sem=self.recv_sems.at[k],
            device_id=target(off),
            device_id_type=MESH,
        )
        copy.start()
        return copy


class GatherTp:
    def __init__(self, send, buf, rows, part):
        self.send, self.buf, self.rows, self.part = send, buf, rows, part
        self.core = place()[4]
        self.done = []
        self.sib = []

    def slot(self, k):
        return self.buf.at[self.core, pl.ds(k * self.rows, self.rows)]

    def go(self, src, dst, h, off):
        copy = self.send(self.part(self.slot(src), h), self.part(self.slot(dst), h), off)
        self.done.append(copy)
        return copy

    def sibling(self, k):
        self.sib.append(self.send(self.slot(k), self.slot(k), CORE))

    def p1(self):
        self.z = [self.go(0, 4, 0, ZH), self.go(0, 4, 1, ZH)]
        self.p0 = self.go(0, 1, 0, YP)
        self.m1 = self.go(0, 2, 1, YM)
        self.p1_ = self.go(0, 1, 1, YP)
        self.m0 = self.go(0, 2, 0, YM)
        self.sibling(0)

    def p2(self):
        self.z[0].wait_recv()
        self.q0 = self.go(4, 5, 0, YP)
        self.z[1].wait_recv()
        self.n1 = self.go(4, 6, 1, YM)
        self.q1 = self.go(4, 5, 1, YP)
        self.n0 = self.go(4, 6, 0, YM)
        self.sibling(4)

    def p3(self):
        self.p0.wait_recv()
        self.f1 = self.go(1, 3, 0, YP)
        self.m1.wait_recv()
        self.f2 = self.go(2, 3, 1, YM)
        self.p1_.wait_recv()
        self.sibling(1)
        self.m0.wait_recv()
        self.sibling(2)
        self.q0.wait_recv()
        self.f3 = self.go(5, 7, 0, YP)
        self.n1.wait_recv()
        self.f4 = self.go(6, 7, 1, YM)

    def p4(self):
        self.f1.wait_recv()
        self.f2.wait_recv()
        self.sibling(3)
        self.q1.wait_recv()
        self.sibling(5)
        self.n0.wait_recv()
        self.sibling(6)
        self.f3.wait_recv()
        self.f4.wait_recv()
        self.sibling(7)

    def p5(self):
        for copy in self.sib:
            copy.wait_recv()
        for copy in self.sib + self.done:
            copy.wait_send()

    def all(self):
        self.p1()
        self.p2()
        self.p3()
        self.p4()
        self.p5()


class GatherRep:
    def __init__(self, send, ref, late_z):
        self.send, self.ref, self.late_z = send, ref, late_z
        self.first, self.second, self.third = {}, {}, {}

    def go(self, src, dst, j, off):
        return [self.send(a, b, off) for a, b in zip(self.ref(src, j), self.ref(dst, j, off))]

    def a(self, j):
        self.first[j] = (self.go(0, 4, j, ZL), self.go(0, 1, j, XP), self.go(0, 2, j, XM))

    def b(self, j):
        for copies in self.first[j]:
            for copy in copies:
                copy.wait_recv()
        f = self.go(1, 3, j, XP) if j % 2 == 0 else self.go(2, 3, j, XM)
        if j not in self.late_z:
            more = (self.go(4, 5, j, XP), self.go(4, 6, j, XM))
        else:
            more = (self.go(1, 5, j, ZL), self.go(2, 6, j, ZL))
        self.second[j] = (f,) + more

    def c(self, j):
        for copies in self.second[j]:
            for copy in copies:
                copy.wait_recv()
        if j not in self.late_z:
            self.third[j] = self.go(5, 7, j, XP) if j % 2 == 1 else self.go(6, 7, j, XM)
        else:
            self.third[j] = self.go(3, 7, j, ZL)

    def end(self, j):
        for copy in self.third[j]:
            copy.wait_recv()
        for copies in self.first[j] + self.second[j] + (self.third[j],):
            for copy in copies:
                copy.wait_send()


def columns_part(ref, h):
    return ref.at[:, pl.ds(h * (HALF // 2), HALF // 2)]


def rows_part(ref, h):
    return ref.at[pl.ds(h * (ROWS // 2), ROWS // 2)]


def body(
    scale_up,
    scale_down,
    pick,
    pool_tokens,
    pool_targets,
    up_hbm,
    down_hbm,
    out,
    up,
    down,
    down_own,
    sib_out,
    sib_prep,
    local,
    tok0,
    tok1,
    pre,
    hid,
    ht0,
    ht1,
    sib_send,
    sib_recv,
    part,
    r_far,
    r_near,
    r_z,
    err0,
    es0,
    es1,
    acc,
    grad0,
    base,
    send_sems,
    recv_sems,
    copy_sems,
):
    _, _, _, _, core = place()
    me = lax.axis_index("rep")
    send = Sends(send_sems, recv_sems)

    loads = [
        pltpu.make_async_copy(up_hbm, up, copy_sems.at[0]),
        pltpu.make_async_copy(down_hbm, down, copy_sems.at[1]),
    ]
    for h in range(2):
        cols = pl.ds(pl.multiple_of(h * HALF + me * SLICE, SLICE), SLICE)
        loads.append(pltpu.make_async_copy(down_hbm.at[:, cols], down_own.at[h], copy_sems.at[2 + h]))
    for load in loads:
        load.start()

    peers = (CORE, YP, YM, ZH) + REP[1:]
    barrier = pltpu.get_barrier_semaphore()
    for off in peers:
        pl.semaphore_signal(barrier, inc=1, device_id=target(off), device_id_type=MESH)

    def picked(step, pool, cols):
        row = lax.broadcasted_iota(jnp.int32, (24, 64), 0)
        col = lax.broadcasted_iota(jnp.int32, (24, 64), 1)
        chosen = jnp.zeros((24, 64), jnp.int32)
        for i in range(24):
            chosen = jnp.where(row == i, pick[step, i], chosen)
        return jnp.dot((chosen == col).astype(F32).astype(BF), pool[:, cols], preferred_element_type=F32)

    sources = [(step, pool) for step in range(2) for pool in (pool_tokens, pool_targets)]

    @pl.loop(0, HALF // 512)
    def _(k):
        inner = pl.ds(pl.multiple_of(k * 512, 512), 512)
        cols = pl.ds(pl.multiple_of((1 - core) * HALF + k * 512, 512), 512)
        sib_out[:, inner] = jnp.concatenate([picked(*source, cols) for source in sources], axis=0).astype(BF)

    pl.semaphore_wait(barrier, len(peers))

    prep = send(sib_out, sib_prep, CORE)
    prep.wait_recv()

    @pl.loop(0, HALF // 512)
    def _(k):
        inner = pl.ds(pl.multiple_of(k * 512, 512), 512)
        cols = pl.ds(pl.multiple_of(core * HALF + k * 512, 512), 512)
        theirs = sib_prep[:, inner].astype(F32)
        for i, source in enumerate(sources):
            a, b = picked(*source, cols), theirs[24 * i : 24 * i + 24]
            first, second = jnp.where(core == 0, a, b), jnp.where(core == 0, b, a)
            local[i, :, inner] = jnp.concatenate([first, second], axis=0).astype(BF)

    prep.wait_send()
    tok0[core, pl.ds(0, TOK), :] = local[0]
    tok1[core, pl.ds(0, TOK), :] = local[2]

    def preact(tokens):
        pre[...] = jnp.zeros_like(pre)
        for h in range(2):

            @pl.loop(0, HALF // 512)
            def _(k):
                cols = pl.ds(pl.multiple_of(k * 512, 512), 512)
                rows = pl.ds(pl.multiple_of(h * HALF + k * 512, 512), 512)
                pre[...] += jnp.dot(tokens[h, :, cols], up[rows, :], preferred_element_type=F32)

    def activate(ht):
        @pl.loop(0, 7)
        def _(k):
            cols = pl.ds(pl.multiple_of(k * 128, 128), 128)
            v = pre[:, cols] * scale_up
            hidden = (v * jax.nn.sigmoid(v)).astype(BF)
            hid[:, cols] = hidden
            ht[0, cols, :] = hidden.T

    def layer_out(base, width, store):
        @pl.loop(0, width // 512)
        def _(k):
            inner = pl.multiple_of(k * 512, 512)
            cols = pl.ds(pl.multiple_of(base + inner, 512), 512)
            store(inner, jnp.dot(hid[...], down[:, cols], preferred_element_type=F32))

    def forward_down(between):
        sib = []
        for h in range(2):

            def to_sibling(inner, value, h=h):
                sib_send[h, :, pl.ds(inner, 512)] = value.astype(BF)

            layer_out((1 - core) * HALF + h * 1024, 1024, to_sibling)
            sib.append(send(sib_send.at[h], sib_recv.at[h], CORE))
        between()
        for h in range(2):
            sib[h].wait_recv()

            def to_part(inner, value, h=h):
                total = value + sib_recv[h, :, pl.ds(inner, 512)].astype(F32)
                part[h, :, pl.ds(inner, 512)] = total.astype(BF)

            layer_out(core * HALF + h * 1024, 1024, to_part)
        for copy in sib:
            copy.wait_send()

    def scatter(hooks=(None, None, None)):
        sent = []

        def go(src, dst, off):
            copy = send(src, dst, off)
            sent.append(copy)
            return copy

        def block(k, h):
            return part.at[h, pl.ds(k * TOK, TOK)]

        far, near = {}, {}
        for p in (1, 0):
            far[p, 0] = go(block(4 * p + 3, 0), r_far.at[p, 0], YP)
            far[p, 1] = go(block(4 * p + 3, 1), r_far.at[p, 1], YM)
            near[p, 0, 1] = go(block(4 * p + 2, 1), r_near.at[p, 0, 1], YP)
            near[p, 1, 0] = go(block(4 * p + 1, 0), r_near.at[p, 1, 0], YM)
        run(hooks[0])
        for p in (1, 0):
            for d, off in ((0, YP), (1, YM)):
                far[p, d].wait_recv()
                rows = pl.ds((4 * p + 2 - d) * TOK, TOK)
                total = part[d, rows, :].astype(F32) + r_far[p, d].astype(F32)
                part[d, rows, :] = total.astype(BF)
                near[p, d, d] = go(block(4 * p + 2 - d, d), r_near.at[p, d, d], off)
        run(hooks[1])
        z = []
        for h in range(2):
            near[1, 0, h].wait_recv()
            near[1, 1, h].wait_recv()
            rows = pl.ds(4 * TOK, TOK)
            total = part[h, rows, :].astype(F32) + r_near[1, 0, h].astype(F32) + r_near[1, 1, h].astype(F32)
            part[h, rows, :] = total.astype(BF)
            z.append(go(block(4, h), r_z.at[h], ZH))
        run(hooks[2])
        halves = []
        for h in range(2):
            near[0, 0, h].wait_recv()
            near[0, 1, h].wait_recv()
            total = part[h, pl.ds(0, TOK), :].astype(F32) + r_near[0, 0, h].astype(F32) + r_near[0, 1, h].astype(F32)
            z[h].wait_recv()
            halves.append(total + r_z[h].astype(F32))
        for copy in sent:
            copy.wait_send()
        return halves

    def error(step, halves, dst, es):
        for h in range(2):
            cols = pl.ds(h * 1024, 1024)
            value = local[2 * step, :, cols].astype(F32) + scale_down * halves[h] - local[2 * step + 1, :, cols].astype(F32)
            dst[:, cols] = value.astype(BF)
        sent = []
        for k in range(1, 8):
            cols = pl.ds(pl.multiple_of(rep_index(REP[k]) * SLICE, SLICE), SLICE)
            sent.append(send(dst.at[:, cols], es.at[core, pl.ds(k * TOK, TOK)], REP[k]))
        cols = pl.ds(pl.multiple_of(me * SLICE, SLICE), SLICE)
        es[core, pl.ds(0, TOK), :] = dst[:, cols]
        return sent

    def hidden_gather(ht):
        size = ht.shape[1] // CHUNKS
        return GatherRep(send, lambda slot, j, off=None: [ht.at[slot, pl.ds(j * size, size)]], (3,))

    GatherTp(send, tok0, TOK, columns_part).all()
    late = GatherTp(send, tok1, TOK, columns_part)
    late.p1()
    loads[0].wait()
    preact(tok0)
    late.p2()
    activate(ht0)
    rep0 = hidden_gather(ht0)
    for j in range(CHUNKS):
        rep0.a(j)
    loads[1].wait()
    forward_down(late.p3)
    halves = scatter()
    late.p4()
    sliced = error(0, halves, err0.at[core, pl.ds(0, TOK)], es0)
    def transpose_tokens(quarter):
        h = quarter // 2

        @pl.loop(0, 4)
        def _(k):
            inner = pl.multiple_of(quarter % 2 * 1024 + k * 256, 256)
            wide = pl.multiple_of(h * HALF + inner, 256)
            turned = tok0[h, :, pl.ds(inner, 256)].T
            grad0[pl.ds(wide, 256), :] = turned[:, :256]
            grad0[pl.ds(2 * HALF + wide, 256), pl.ds(0, 128)] = turned[:, 256:]

    gather = GatherTp(send, err0, TOK, columns_part)
    gather.p1()
    transpose_tokens(0)
    for j in range(CHUNKS):
        rep0.b(j)
    gather.p2()
    transpose_tokens(1)
    gather.p3()
    transpose_tokens(2)
    gather.p4()
    transpose_tokens(3)
    gather.p5()
    for copy in sliced:
        copy.wait()
    slices = GatherTp(send, es0, ROWS, rows_part)
    slices.p1()

    acc[...] = jnp.zeros_like(acc)
    for h in range(2):

        @pl.loop(0, HALF // 512)
        def _(k):
            cols = pl.ds(pl.multiple_of(k * 512, 512), 512)
            wide = pl.ds(pl.multiple_of(h * HALF + k * 512, 512), 512)
            acc[...] += lax.dot_general(
                err0[h, :, cols], down[:, wide], (((1,), (1,)), ((), ())), preferred_element_type=F32
            )

    @pl.loop(0, 3)
    def _(n):
        rows = pl.ds(pl.multiple_of(n * 128, 128), 128)
        v = pre[rows, :] * scale_up
        sigma = jax.nn.sigmoid(v)
        hid[rows, :] = (scale_down * acc[rows, :] * (sigma * (1.0 + v * (1.0 - sigma)))).astype(BF)

    slices.p2()
    for h in range(2):

        @pl.loop(0, HALF // 256)
        def _(k):
            wide = pl.multiple_of(h * HALF + k * 256, 256)
            rows = pl.ds(wide, 256)
            g = jnp.dot(grad0[rows, :], hid[pl.ds(0, 256), :], preferred_element_type=F32)
            g += jnp.dot(
                grad0[pl.ds(2 * HALF + wide, 256), pl.ds(0, 128)], hid[pl.ds(256, 128), :], preferred_element_type=F32
            )
            u = g * inverse(jnp.abs(g) + 0.02 / scale_up)
            up[rows, :] = (0.975 * up[rows, :].astype(F32) - 0.25 * u).astype(BF)

    slices.p3()
    for j in range(CHUNKS):
        rep0.c(j)
    late.p5()

    preact(tok1)
    activate(ht1)
    rep1 = hidden_gather(ht1)
    for j in range(CHUNKS):
        rep1.a(j)
    for h in range(2):

        @pl.loop(0, HALF // 256)
        def _(k):
            cols = pl.ds(pl.multiple_of(k * 256, 256), 256)
            wide = pl.ds(pl.multiple_of(h * HALF + k * 256, 256), 256)
            g = jnp.dot(ht0[0], err0[h, :, cols], preferred_element_type=F32)
            u = g * inverse(jnp.abs(g) + 0.02 / scale_down)
            down[:, wide] = (0.975 * down[:, wide].astype(F32) - 0.25 * u).astype(BF)

    slices.p4()
    for j in range(CHUNKS):
        rep0.end(j)

    es0_view = es0.reshape(2, 8, ROWS, SLICE)
    es1_view = es1.reshape(2, 8, ROWS, SLICE)
    size = 896 // CHUNKS

    def slice_of(view, h, k):
        tokens = pl.ds(k * TOK if isinstance(k, int) else pl.multiple_of(k * TOK, TOK), TOK)
        return view[h, :, tokens, :].reshape(ROWS, SLICE)

    def first_update(k):
        for h in range(2):
            e = slice_of(es0_view, h, k)

            @pl.loop(0, CHUNKS)
            def _(j):
                rows = pl.ds(pl.multiple_of(j * size, size), size)
                kept = pl.ds(pl.multiple_of((k * 2 + h) * 896 + j * size, 32), size)
                g = jnp.dot(ht0[k, rows, :], e, preferred_element_type=F32)
                u = g * inverse(jnp.abs(g) + 0.02 / scale_down)
                grad0[kept, :] = g.astype(BF)
                if k == 0:
                    base[h, rows, :] = 0.975 * u
                else:
                    base[h, rows, :] += 0.975 * u

    def both(k, then=None):
        def hook():
            first_update(k)
            run(then)

        return hook

    forward_down(slices.p5)
    rep1.b(0)
    halves = scatter((both(0, lambda: rep1.b(1)), both(1, lambda: rep1.b(2)), both(2, lambda: rep1.b(3))))
    sliced = error(1, halves, local.at[0], es1)
    rep1.c(0)
    first_update(3)
    for copy in sliced:
        copy.wait()
    last = GatherTp(send, es1, ROWS, rows_part)
    last.p1()
    rep1.c(1)
    first_update(4)
    last.p2()
    rep1.c(2)
    first_update(5)
    last.p3()
    rep1.c(3)
    first_update(6)
    last.p4()
    first_update(7)
    last.p5()
    for j in range(CHUNKS):
        rep1.end(j)
    loads[2].wait()
    loads[3].wait()

    def reduce(j, h):
        rows = pl.ds(j * size, size)

        def one(k, total):
            g0 = grad0[pl.ds(pl.multiple_of((k * 2 + h) * 896 + j * size, 32), size), :].astype(F32)
            g1 = jnp.dot(ht1[k, rows, :], slice_of(es1_view, h, k), preferred_element_type=F32)
            first = (0.09 / 0.19) * g0 + (0.1 / 0.19) * g1
            second = (0.0475 / 0.0975) * (g0 * g0) + (0.05 / 0.0975) * (g1 * g1)
            root = second * lax.rsqrt(jnp.maximum(second, 1e-30))
            return total + first * inverse(root + 0.02 / scale_down)

        total = lax.fori_loop(0, 8, one, base[h, rows, :])
        w = down_own[h, rows, :].astype(F32)
        average = (1.0 - 0.975 * 0.975) * w + (0.25 / 8.0) * total
        down_own[h, rows, :] = (w - 0.7 * 1.9 * average).astype(BF)

    def pieces(slot, n, off=None):
        h, rows = n // CHUNKS, pl.ds(n % CHUNKS * size, size)
        if slot == 0:
            return [down_own.at[h, rows]]
        back = REP[slot]
        shift = off if off is not None else (0, 0)
        r = rep_index((shift[0] - back[0] + 4, shift[1] - back[1] + 2))
        return [out.at[rows, pl.ds(pl.multiple_of(h * HALF + r * SLICE, SLICE), SLICE)]]

    final = GatherRep(send, pieces, (0, 3, 6))
    own = []
    total = 2 * CHUNKS
    for n in range(total + LAG_C):
        if n < total:
            h, j = n // CHUNKS, n % CHUNKS
            reduce(j, h)
            final.a(n)
            cols = pl.ds(pl.multiple_of(h * HALF + me * SLICE, SLICE), SLICE)
            rows = pl.ds(j * size, size)
            own.append(pltpu.make_async_copy(down_own.at[h, rows], out.at[rows, cols], copy_sems.at[4 + n]))
            own[-1].start()
        if 0 <= n - LAG_B < total:
            final.b(n - LAG_B)
        if 0 <= n - LAG_C < total:
            final.c(n - LAG_C)
    for n in range(total):
        final.end(n)
    for copy in own:
        copy.wait()


LAG_B, LAG_C = 1, 2
SEMS = 300


def round_kernel(pick, pool_tokens, pool_targets, up_weight, down_weight, scale_up, scale_down):
    vmem, anywhere = pl.BlockSpec(memory_space=pltpu.VMEM), pl.BlockSpec(memory_space=pl.ANY)
    width, hidden = up_weight.shape
    return pl.pallas_call(
        functools.partial(body, scale_up, scale_down),
        out_shape=jax.ShapeDtypeStruct(down_weight.shape, BF),
        in_specs=[pl.BlockSpec(memory_space=pltpu.SMEM), vmem, vmem, anywhere, anywhere],
        out_specs=anywhere,
        scratch_shapes=[
            pltpu.VMEM((width, hidden), BF),
            pltpu.VMEM((hidden, width), BF),
            pltpu.VMEM((2, hidden, SLICE), BF),
            pltpu.VMEM((96, HALF), BF),
            pltpu.VMEM((96, HALF), BF),
            pltpu.VMEM((4, TOK, HALF), BF),
            pltpu.VMEM((2, ROWS, HALF), BF),
            pltpu.VMEM((2, ROWS, HALF), BF),
            pltpu.VMEM((ROWS, hidden), F32),
            pltpu.VMEM((ROWS, hidden), BF),
            pltpu.VMEM((8, hidden, ROWS), BF),
            pltpu.VMEM((8, hidden, ROWS), BF),
            pltpu.VMEM((2, ROWS, HALF // 2), BF),
            pltpu.VMEM((2, ROWS, HALF // 2), BF),
            pltpu.VMEM((2, ROWS, HALF // 2), BF),
            pltpu.VMEM((2, 2, TOK, HALF // 2), BF),
            pltpu.VMEM((2, 2, 2, TOK, HALF // 2), BF),
            pltpu.VMEM((2, TOK, HALF // 2), BF),
            pltpu.VMEM((2, ROWS, HALF), BF),
            pltpu.VMEM((2, 8 * ROWS, SLICE), BF),
            pltpu.VMEM((2, 8 * ROWS, SLICE), BF),
            pltpu.VMEM((ROWS, hidden), F32),
            pltpu.VMEM((16 * hidden, SLICE), BF),
            pltpu.VMEM((2, hidden, SLICE), F32),
            pltpu.SemaphoreType.DMA((SEMS,)),
            pltpu.SemaphoreType.DMA((SEMS,)),
            pltpu.SemaphoreType.DMA((4 + 2 * CHUNKS,)),
        ],
        compiler_params=pltpu.CompilerParams(
            collective_id=0, has_side_effects=True, vmem_limit_bytes=62 * 2**20
        ),
    )(pick, pool_tokens, pool_targets, up_weight, down_weight)


def per_device(pool_tokens, pool_targets, pick, up_weight, down_weight):
    scale_up = 1.0 / math.sqrt(up_weight.shape[0])
    scale_down = 1.0 / math.sqrt(up_weight.shape[1] * lax.axis_size("tp"))
    return round_kernel(pick[0], pool_tokens, pool_targets, up_weight, down_weight, scale_up, scale_down)


def solution(mesh):
    in_specs = (P("tp", None), P("tp", None), P("rep", None, "tp"), P(None, "tp"), P("tp", None))
    return jax.shard_map(per_device, mesh=mesh, in_specs=in_specs, out_specs=P("tp", None), check_vma=False)
```

```python
import functools
import math

import jax
import jax.numpy as jnp
from jax import lax
from jax.experimental import pallas as pl
from jax.experimental.pallas import tpu as pltpu
from jax.sharding import PartitionSpec as P

MESH = pl.DeviceIdType.MESH
BF, F32 = jnp.bfloat16, jnp.float32

CORE = (0, 0, 0, 0, 1)
YP, YM = (0, 0, 0, 1, 0), (0, 0, 0, -1, 0)
ZH = (0, 0, 1, 0, 0)
XP, XM, X2, ZL = (1, 0, 0, 0, 0), (-1, 0, 0, 0, 0), (2, 0, 0, 0, 0), (0, 1, 0, 0, 0)
REP = (None, XP, XM, X2, ZL, (1, 1, 0, 0, 0), (-1, 1, 0, 0, 0), (2, 1, 0, 0, 0))

TOK = 48
HALF = 2048
ROWS = 384
SLICE = 256
CHUNKS = 4


def place():
    r, t = lax.axis_index("rep"), lax.axis_index("tp")
    return r // 2, r % 2, t // 8, (t // 2) % 4, t % 2


def rep_index(off):
    x, zl, _, _, _ = place()
    return ((x + off[0] + 4) % 4) * 2 + (zl + off[1]) % 2


def target(off):
    _, _, zh, y, core = place()
    tp = (((zh + off[2]) % 2) * 4 + (y + off[3] + 4) % 4) * 2 + (core + off[4]) % 2
    return (rep_index(off), tp)


def inverse(v):
    return pl.reciprocal(v, approx=True)


def run(hook):
    if hook is not None:
        hook()


class Sends:
    def __init__(self, send_sems, recv_sems):
        self.send_sems, self.recv_sems, self.count = send_sems, recv_sems, 0

    def __call__(self, src, dst, off):
        k = self.count
        self.count += 1
        copy = pltpu.make_async_remote_copy(
            src_ref=src,
            dst_ref=dst,
            send_sem=self.send_sems.at[k],
            recv_sem=self.recv_sems.at[k],
            device_id=target(off),
            device_id_type=MESH,
        )
        copy.start()
        return copy


class GatherTp:
    def __init__(self, send, buf, rows, part):
        self.send, self.buf, self.rows, self.part = send, buf, rows, part
        self.core = place()[4]
        self.done = []
        self.sib = []

    def slot(self, k):
        return self.buf.at[self.core, pl.ds(k * self.rows, self.rows)]

    def go(self, src, dst, h, off):
        copy = self.send(self.part(self.slot(src), h), self.part(self.slot(dst), h), off)
        self.done.append(copy)
        return copy

    def sibling(self, k):
        self.sib.append(self.send(self.slot(k), self.slot(k), CORE))

    def p1(self):
        self.z = [self.go(0, 4, 0, ZH), self.go(0, 4, 1, ZH)]
        self.p0 = self.go(0, 1, 0, YP)
        self.m1 = self.go(0, 2, 1, YM)
        self.p1_ = self.go(0, 1, 1, YP)
        self.m0 = self.go(0, 2, 0, YM)
        self.sibling(0)

    def p2(self):
        self.z[0].wait_recv()
        self.q0 = self.go(4, 5, 0, YP)
        self.z[1].wait_recv()
        self.n1 = self.go(4, 6, 1, YM)
        self.q1 = self.go(4, 5, 1, YP)
        self.n0 = self.go(4, 6, 0, YM)
        self.sibling(4)

    def p3(self):
        self.p0.wait_recv()
        self.f1 = self.go(1, 3, 0, YP)
        self.m1.wait_recv()
        self.f2 = self.go(2, 3, 1, YM)
        self.p1_.wait_recv()
        self.sibling(1)
        self.m0.wait_recv()
        self.sibling(2)
        self.q0.wait_recv()
        self.f3 = self.go(5, 7, 0, YP)
        self.n1.wait_recv()
        self.f4 = self.go(6, 7, 1, YM)

    def p4(self):
        self.f1.wait_recv()
        self.f2.wait_recv()
        self.sibling(3)
        self.q1.wait_recv()
        self.sibling(5)
        self.n0.wait_recv()
        self.sibling(6)
        self.f3.wait_recv()
        self.f4.wait_recv()
        self.sibling(7)

    def p5(self):
        for copy in self.sib:
            copy.wait_recv()
        for copy in self.sib + self.done:
            copy.wait_send()

    def all(self):
        self.p1()
        self.p2()
        self.p3()
        self.p4()
        self.p5()


class GatherRep:
    def __init__(self, send, ref, late_z):
        self.send, self.ref, self.late_z = send, ref, late_z
        self.first, self.second, self.third = {}, {}, {}

    def go(self, src, dst, j, off):
        return [self.send(a, b, off) for a, b in zip(self.ref(src, j), self.ref(dst, j, off))]

    def a(self, j):
        self.first[j] = (self.go(0, 4, j, ZL), self.go(0, 1, j, XP), self.go(0, 2, j, XM))

    def b(self, j):
        for copies in self.first[j]:
            for copy in copies:
                copy.wait_recv()
        f = self.go(1, 3, j, XP) if j % 2 == 0 else self.go(2, 3, j, XM)
        if j not in self.late_z:
            more = (self.go(4, 5, j, XP), self.go(4, 6, j, XM))
        else:
            more = (self.go(1, 5, j, ZL), self.go(2, 6, j, ZL))
        self.second[j] = (f,) + more

    def c(self, j):
        for copies in self.second[j]:
            for copy in copies:
                copy.wait_recv()
        if j not in self.late_z:
            self.third[j] = self.go(5, 7, j, XP) if j % 2 == 1 else self.go(6, 7, j, XM)
        else:
            self.third[j] = self.go(3, 7, j, ZL)

    def end(self, j):
        for copy in self.third[j]:
            copy.wait_recv()
        for copies in self.first[j] + self.second[j] + (self.third[j],):
            for copy in copies:
                copy.wait_send()


def columns_part(ref, h):
    return ref.at[:, pl.ds(h * (HALF // 2), HALF // 2)]


def rows_part(ref, h):
    return ref.at[pl.ds(h * (ROWS // 2), ROWS // 2)]


def body(
    scale_up,
    scale_down,
    pick,
    pool_tokens,
    pool_targets,
    up_hbm,
    down_hbm,
    out,
    up,
    down,
    down_own,
    local,
    tok0,
    tok1,
    pre,
    hid,
    ht0,
    ht1,
    sib_send,
    sib_recv,
    part,
    r_far,
    r_near,
    r_z,
    err0,
    es0,
    es1,
    acc,
    grad0,
    base,
    send_sems,
    recv_sems,
    copy_sems,
):
    _, _, _, _, core = place()
    me = lax.axis_index("rep")
    send = Sends(send_sems, recv_sems)

    loads = [
        pltpu.make_async_copy(up_hbm, up, copy_sems.at[0]),
        pltpu.make_async_copy(down_hbm, down, copy_sems.at[1]),
    ]
    for h in range(2):
        cols = pl.ds(pl.multiple_of(h * HALF + me * SLICE, SLICE), SLICE)
        loads.append(pltpu.make_async_copy(down_hbm.at[:, cols], down_own.at[h], copy_sems.at[2 + h]))
    for load in loads:
        load.start()

    peers = (CORE, YP, YM, ZH) + REP[1:]
    barrier = pltpu.get_barrier_semaphore()
    for off in peers:
        pl.semaphore_signal(barrier, inc=1, device_id=target(off), device_id_type=MESH)

    def picked(step, pool, cols):
        row = lax.broadcasted_iota(jnp.int32, (24, 64), 0)
        col = lax.broadcasted_iota(jnp.int32, (24, 64), 1)
        chosen = jnp.zeros((24, 64), jnp.int32)
        for i in range(24):
            chosen = jnp.where(row == i, pick[step, i], chosen)
        return jnp.dot((chosen == col).astype(F32).astype(BF), pool[:, cols], preferred_element_type=F32)

    sources = [(step, pool) for step in range(2) for pool in (pool_tokens, pool_targets)]

    @pl.loop(0, HALF // 512)
    def _(k):
        inner = pl.ds(pl.multiple_of(k % 2 * 512, 512), 512)
        cols = pl.ds(pl.multiple_of((1 - core) * HALF + k * 512, 512), 512)
        part[k // 2, pl.ds(0, 96), inner] = jnp.concatenate([picked(*source, cols) for source in sources], axis=0).astype(BF)

    pl.semaphore_wait(barrier, len(peers))

    prep = send(part.at[:, pl.ds(0, 96)], sib_recv.at[:, pl.ds(0, 96)], CORE)
    prep.wait_recv()

    @pl.loop(0, HALF // 512)
    def _(k):
        inner = pl.ds(pl.multiple_of(k * 512, 512), 512)
        cols = pl.ds(pl.multiple_of(core * HALF + k * 512, 512), 512)
        theirs = sib_recv[k // 2, pl.ds(0, 96), pl.ds(pl.multiple_of(k % 2 * 512, 512), 512)].astype(F32)
        for i, source in enumerate(sources):
            a, b = picked(*source, cols), theirs[24 * i : 24 * i + 24]
            first, second = jnp.where(core == 0, a, b), jnp.where(core == 0, b, a)
            local[i, :, inner] = jnp.concatenate([first, second], axis=0).astype(BF)

    prep.wait_send()
    tok0[core, pl.ds(0, TOK), :] = local[0]
    tok1[core, pl.ds(0, TOK), :] = local[2]

    def preact(tokens):
        pre[...] = jnp.zeros_like(pre)
        for h in range(2):

            @pl.loop(0, HALF // 1024, unroll=2)
            def _(k):
                cols = pl.ds(pl.multiple_of(k * 1024, 1024), 1024)
                rows = pl.ds(pl.multiple_of(h * HALF + k * 1024, 1024), 1024)
                pre[...] += jnp.dot(tokens[h, :, cols], up[rows, :], preferred_element_type=F32)

    def activate(ht):
        @pl.loop(0, 7)
        def _(k):
            cols = pl.ds(pl.multiple_of(k * 128, 128), 128)
            v = pre[:, cols] * scale_up
            hidden = (v * jax.nn.sigmoid(v)).astype(BF)
            hid[:, cols] = hidden
            ht[0, cols, :] = hidden.T

    def layer_out(base, width, store):
        @pl.loop(0, width // 512, unroll=2)
        def _(k):
            inner = pl.multiple_of(k * 512, 512)
            cols = pl.ds(pl.multiple_of(base + inner, 512), 512)
            store(inner, jnp.dot(hid[...], down[:, cols], preferred_element_type=F32))

    def forward_down(between):
        sib = []
        for h in range(2):

            def to_sibling(inner, value, h=h):
                sib_send[h, :, pl.ds(inner, 512)] = value.astype(BF)

            layer_out((1 - core) * HALF + h * 1024, 1024, to_sibling)
            sib.append(send(sib_send.at[h], sib_recv.at[h], CORE))
        between()
        for h in range(2):
            sib[h].wait_recv()

            def to_part(inner, value, h=h):
                total = value + sib_recv[h, :, pl.ds(inner, 512)].astype(F32)
                part[h, :, pl.ds(inner, 512)] = total.astype(BF)

            layer_out(core * HALF + h * 1024, 1024, to_part)
        for copy in sib:
            copy.wait_send()

    def scatter(hooks=(None, None, None)):
        sent = []

        def go(src, dst, off):
            copy = send(src, dst, off)
            sent.append(copy)
            return copy

        def block(k, h):
            return part.at[h, pl.ds(k * TOK, TOK)]

        far, near = {}, {}
        for p in (1, 0):
            far[p, 0] = go(block(4 * p + 3, 0), r_far.at[p, 0], YP)
            far[p, 1] = go(block(4 * p + 3, 1), r_far.at[p, 1], YM)
            near[p, 0, 1] = go(block(4 * p + 2, 1), r_near.at[p, 0, 1], YP)
            near[p, 1, 0] = go(block(4 * p + 1, 0), r_near.at[p, 1, 0], YM)
        run(hooks[0])
        for p in (1, 0):
            for d, off in ((0, YP), (1, YM)):
                far[p, d].wait_recv()
                rows = pl.ds((4 * p + 2 - d) * TOK, TOK)
                total = part[d, rows, :].astype(F32) + r_far[p, d].astype(F32)
                part[d, rows, :] = total.astype(BF)
                near[p, d, d] = go(block(4 * p + 2 - d, d), r_near.at[p, d, d], off)
        run(hooks[1])
        z = []
        for h in range(2):
            near[1, 0, h].wait_recv()
            near[1, 1, h].wait_recv()
            rows = pl.ds(4 * TOK, TOK)
            total = part[h, rows, :].astype(F32) + r_near[1, 0, h].astype(F32) + r_near[1, 1, h].astype(F32)
            part[h, rows, :] = total.astype(BF)
            z.append(go(block(4, h), r_z.at[h], ZH))
        run(hooks[2])
        halves = []
        for h in range(2):
            near[0, 0, h].wait_recv()
            near[0, 1, h].wait_recv()
            total = part[h, pl.ds(0, TOK), :].astype(F32) + r_near[0, 0, h].astype(F32) + r_near[0, 1, h].astype(F32)
            z[h].wait_recv()
            halves.append(total + r_z[h].astype(F32))
        for copy in sent:
            copy.wait_send()
        return halves

    def error(step, halves, dst, es):
        for h in range(2):
            cols = pl.ds(h * 1024, 1024)
            value = local[2 * step, :, cols].astype(F32) + scale_down * halves[h] - local[2 * step + 1, :, cols].astype(F32)
            dst[:, cols] = value.astype(BF)
        sent = []
        for k in range(1, 8):
            cols = pl.ds(pl.multiple_of(rep_index(REP[k]) * SLICE, SLICE), SLICE)
            sent.append(send(dst.at[:, cols], es.at[core, pl.ds(k * TOK, TOK)], REP[k]))
        cols = pl.ds(pl.multiple_of(me * SLICE, SLICE), SLICE)
        es[core, pl.ds(0, TOK), :] = dst[:, cols]
        return sent

    def hidden_gather(ht):
        size = ht.shape[1] // CHUNKS
        return GatherRep(send, lambda slot, j, off=None: [ht.at[slot, pl.ds(j * size, size)]], (3,))

    GatherTp(send, tok0, TOK, columns_part).all()
    late = GatherTp(send, tok1, TOK, columns_part)
    late.p1()
    loads[0].wait()
    preact(tok0)
    late.p2()
    activate(ht0)
    rep0 = hidden_gather(ht0)
    for j in range(CHUNKS):
        rep0.a(j)
    loads[1].wait()
    forward_down(late.p3)
    halves = scatter()
    late.p4()
    sliced = error(0, halves, err0.at[core, pl.ds(0, TOK)], es0)
    def transpose_tokens(quarter):
        h = quarter // 2

        @pl.loop(0, 4)
        def _(k):
            inner = pl.multiple_of(quarter % 2 * 1024 + k * 256, 256)
            wide = pl.multiple_of(h * HALF + inner, 256)
            turned = tok0[h, :, pl.ds(inner, 256)].T
            grad0[pl.ds(wide, 256), :] = turned[:, :256]
            grad0[pl.ds(2 * HALF + wide, 256), pl.ds(0, 128)] = turned[:, 256:]

    gather = GatherTp(send, err0, TOK, columns_part)
    gather.p1()
    transpose_tokens(0)
    for j in range(CHUNKS):
        rep0.b(j)
    gather.p2()
    transpose_tokens(1)
    gather.p3()
    transpose_tokens(2)
    gather.p4()
    transpose_tokens(3)
    gather.p5()
    for copy in sliced:
        copy.wait()
    slices = GatherTp(send, es0, ROWS, rows_part)
    slices.p1()

    acc[...] = jnp.zeros_like(acc)
    for h in range(2):

        @pl.loop(0, HALF // 1024, unroll=2)
        def _(k):
            cols = pl.ds(pl.multiple_of(k * 1024, 1024), 1024)
            wide = pl.ds(pl.multiple_of(h * HALF + k * 1024, 1024), 1024)
            acc[...] += lax.dot_general(
                err0[h, :, cols], down[:, wide], (((1,), (1,)), ((), ())), preferred_element_type=F32
            )

    @pl.loop(0, 3)
    def _(n):
        rows = pl.ds(pl.multiple_of(n * 128, 128), 128)
        v = pre[rows, :] * scale_up
        sigma = jax.nn.sigmoid(v)
        hid[rows, :] = (scale_down * acc[rows, :] * (sigma * (1.0 + v * (1.0 - sigma)))).astype(BF)

    slices.p2()
    for h in range(2):

        @pl.loop(0, HALF // 256, unroll=2)
        def _(k):
            wide = pl.multiple_of(h * HALF + k * 256, 256)
            rows = pl.ds(wide, 256)
            g = jnp.dot(grad0[rows, :], hid[pl.ds(0, 256), :], preferred_element_type=F32)
            g += jnp.dot(
                grad0[pl.ds(2 * HALF + wide, 256), pl.ds(0, 128)], hid[pl.ds(256, 128), :], preferred_element_type=F32
            )
            u = g * inverse(jnp.abs(g) + 0.02 / scale_up)
            up[rows, :] = (0.975 * up[rows, :].astype(F32) - 0.25 * u).astype(BF)

    slices.p3()
    for j in range(CHUNKS):
        rep0.c(j)
    late.p5()

    preact(tok1)
    activate(ht1)
    rep1 = hidden_gather(ht1)
    for j in range(CHUNKS):
        rep1.a(j)
    for h in range(2):

        @pl.loop(0, HALF // 256, unroll=2)
        def _(k):
            cols = pl.ds(pl.multiple_of(k * 256, 256), 256)
            wide = pl.ds(pl.multiple_of(h * HALF + k * 256, 256), 256)
            g = jnp.dot(ht0[0], err0[h, :, cols], preferred_element_type=F32)
            u = g * inverse(jnp.abs(g) + 0.02 / scale_down)
            down[:, wide] = (0.975 * down[:, wide].astype(F32) - 0.25 * u).astype(BF)

    slices.p4()
    for j in range(CHUNKS):
        rep0.end(j)

    es0_view = es0.reshape(2, 8, ROWS, SLICE)
    es1_view = es1.reshape(2, 8, ROWS, SLICE)
    size = 896 // CHUNKS

    def slice_of(view, h, k):
        tokens = pl.ds(k * TOK if isinstance(k, int) else pl.multiple_of(k * TOK, TOK), TOK)
        return view[h, :, tokens, :].reshape(ROWS, SLICE)

    def first_update(k):
        for h in range(2):
            e = slice_of(es0_view, h, k)

            @pl.loop(0, CHUNKS)
            def _(j):
                rows = pl.ds(pl.multiple_of(j * size, size), size)
                kept = pl.ds(pl.multiple_of((k * 2 + h) * 896 + j * size, 32), size)
                g = jnp.dot(ht0[k, rows, :], e, preferred_element_type=F32)
                u = g * inverse(jnp.abs(g) + 0.02 / scale_down)
                grad0[kept, :] = g.astype(BF)
                if k == 0:
                    base[h, rows, :] = 0.975 * u
                else:
                    base[h, rows, :] += 0.975 * u

    def both(k, then=None):
        def hook():
            first_update(k)
            run(then)

        return hook

    forward_down(slices.p5)
    rep1.b(0)
    halves = scatter((both(0, lambda: rep1.b(1)), both(1, lambda: rep1.b(2)), both(2, lambda: rep1.b(3))))
    sliced = error(1, halves, local.at[0], es1)
    rep1.c(0)
    first_update(3)
    for copy in sliced:
        copy.wait()
    last = GatherTp(send, es1, ROWS, rows_part)
    last.p1()
    rep1.c(1)
    first_update(4)
    last.p2()
    rep1.c(2)
    first_update(5)
    last.p3()
    rep1.c(3)
    first_update(6)
    last.p4()
    first_update(7)
    last.p5()
    for j in range(CHUNKS):
        rep1.end(j)
    loads[2].wait()
    loads[3].wait()

    def reduce(j, h):
        rows = pl.ds(j * size, size)

        def one(k, total):
            g0 = grad0[pl.ds(pl.multiple_of((k * 2 + h) * 896 + j * size, 32), size), :].astype(F32)
            g1 = jnp.dot(ht1[k, rows, :], slice_of(es1_view, h, k), preferred_element_type=F32)
            first = (0.09 / 0.19) * g0 + (0.1 / 0.19) * g1
            second = (0.0475 / 0.0975) * (g0 * g0) + (0.05 / 0.0975) * (g1 * g1)
            root = second * lax.rsqrt(jnp.maximum(second, 1e-30))
            return total + first * inverse(root + 0.02 / scale_down)

        total = lax.fori_loop(0, 8, one, base[h, rows, :], unroll=2)
        w = down_own[h, rows, :].astype(F32)
        average = (1.0 - 0.975 * 0.975) * w + (0.25 / 8.0) * total
        down_own[h, rows, :] = (w - 0.7 * 1.9 * average).astype(BF)

    def pieces(slot, n, off=None):
        h, rows = n // CHUNKS, pl.ds(n % CHUNKS * size, size)
        if slot == 0:
            return [down_own.at[h, rows]]
        back = REP[slot]
        shift = off if off is not None else (0, 0)
        r = rep_index((shift[0] - back[0] + 4, shift[1] - back[1] + 2))
        return [out.at[rows, pl.ds(pl.multiple_of(h * HALF + r * SLICE, SLICE), SLICE)]]

    final = GatherRep(send, pieces, (0, 3, 6))
    own = []
    total = 2 * CHUNKS
    for n in range(total + LAG_C):
        if n < total:
            h, j = n // CHUNKS, n % CHUNKS
            reduce(j, h)
            final.a(n)
            cols = pl.ds(pl.multiple_of(h * HALF + me * SLICE, SLICE), SLICE)
            rows = pl.ds(j * size, size)
            own.append(pltpu.make_async_copy(down_own.at[h, rows], out.at[rows, cols], copy_sems.at[4 + n]))
            own[-1].start()
        if 0 <= n - LAG_B < total:
            final.b(n - LAG_B)
        if 0 <= n - LAG_C < total:
            final.c(n - LAG_C)
    for n in range(total):
        final.end(n)
    for copy in own:
        copy.wait()


LAG_B, LAG_C = 2, 3
SEMS = 300


def round_kernel(pick, pool_tokens, pool_targets, up_weight, down_weight, scale_up, scale_down):
    vmem, anywhere = pl.BlockSpec(memory_space=pltpu.VMEM), pl.BlockSpec(memory_space=pl.ANY)
    width, hidden = up_weight.shape
    return pl.pallas_call(
        functools.partial(body, scale_up, scale_down),
        out_shape=jax.ShapeDtypeStruct(down_weight.shape, BF),
        in_specs=[pl.BlockSpec(memory_space=pltpu.SMEM), vmem, vmem, anywhere, anywhere],
        out_specs=anywhere,
        scratch_shapes=[
            pltpu.VMEM((width, hidden), BF),
            pltpu.VMEM((hidden, width), BF),
            pltpu.VMEM((2, hidden, SLICE), BF),
            pltpu.VMEM((4, TOK, HALF), BF),
            pltpu.VMEM((2, ROWS, HALF), BF),
            pltpu.VMEM((2, ROWS, HALF), BF),
            pltpu.VMEM((ROWS, hidden), F32),
            pltpu.VMEM((ROWS, hidden), BF),
            pltpu.VMEM((8, hidden, ROWS), BF),
            pltpu.VMEM((8, hidden, ROWS), BF),
            pltpu.VMEM((2, ROWS, HALF // 2), BF),
            pltpu.VMEM((2, ROWS, HALF // 2), BF),
            pltpu.VMEM((2, ROWS, HALF // 2), BF),
            pltpu.VMEM((2, 2, TOK, HALF // 2), BF),
            pltpu.VMEM((2, 2, 2, TOK, HALF // 2), BF),
            pltpu.VMEM((2, TOK, HALF // 2), BF),
            pltpu.VMEM((2, ROWS, HALF), BF),
            pltpu.VMEM((2, 8 * ROWS, SLICE), BF),
            pltpu.VMEM((2, 8 * ROWS, SLICE), BF),
            pltpu.VMEM((ROWS, hidden), F32),
            pltpu.VMEM((16 * hidden, SLICE), BF),
            pltpu.VMEM((2, hidden, SLICE), F32),
            pltpu.SemaphoreType.DMA((SEMS,)),
            pltpu.SemaphoreType.DMA((SEMS,)),
            pltpu.SemaphoreType.DMA((4 + 2 * CHUNKS,)),
        ],
        compiler_params=pltpu.CompilerParams(
            collective_id=0, has_side_effects=True, vmem_limit_bytes=63 * 2**20
        ),
    )(pick, pool_tokens, pool_targets, up_weight, down_weight)


def per_device(pool_tokens, pool_targets, pick, up_weight, down_weight):
    scale_up = 1.0 / math.sqrt(up_weight.shape[0])
    scale_down = 1.0 / math.sqrt(up_weight.shape[1] * lax.axis_size("tp"))
    return round_kernel(pick[0], pool_tokens, pool_targets, up_weight, down_weight, scale_up, scale_down)


def solution(mesh):
    in_specs = (P("tp", None), P("tp", None), P("rep", None, "tp"), P(None, "tp"), P("tp", None))
    return jax.shard_map(per_device, mesh=mesh, in_specs=in_specs, out_specs=P("tp", None), check_vma=False)
```

```python
import functools
import math

import jax
import jax.numpy as jnp
from jax import lax
from jax.experimental import pallas as pl
from jax.experimental.pallas import tpu as pltpu
from jax.sharding import PartitionSpec as P

MESH = pl.DeviceIdType.MESH
BF, F32 = jnp.bfloat16, jnp.float32

CORE = (0, 0, 0, 0, 1)
YP, YM = (0, 0, 0, 1, 0), (0, 0, 0, -1, 0)
ZH = (0, 0, 1, 0, 0)
XP, XM, X2, ZL = (1, 0, 0, 0, 0), (-1, 0, 0, 0, 0), (2, 0, 0, 0, 0), (0, 1, 0, 0, 0)
REP = (None, XP, XM, X2, ZL, (1, 1, 0, 0, 0), (-1, 1, 0, 0, 0), (2, 1, 0, 0, 0))

TOK = 48
HALF = 2048
ROWS = 384
SLICE = 256
CHUNKS = 4


def place():
    r, t = lax.axis_index("rep"), lax.axis_index("tp")
    return r // 2, r % 2, t // 8, (t // 2) % 4, t % 2


def rep_index(off):
    x, zl, _, _, _ = place()
    return ((x + off[0] + 4) % 4) * 2 + (zl + off[1]) % 2


def target(off):
    _, _, zh, y, core = place()
    tp = (((zh + off[2]) % 2) * 4 + (y + off[3] + 4) % 4) * 2 + (core + off[4]) % 2
    return (rep_index(off), tp)


def inverse(v):
    return pl.reciprocal(v, approx=True)


def run(hook):
    if hook is not None:
        hook()


class Sends:
    def __init__(self, send_sems, recv_sems):
        self.send_sems, self.recv_sems, self.count = send_sems, recv_sems, 0

    def __call__(self, src, dst, off):
        k = self.count
        self.count += 1
        copy = pltpu.make_async_remote_copy(
            src_ref=src,
            dst_ref=dst,
            send_sem=self.send_sems.at[k],
            recv_sem=self.recv_sems.at[k],
            device_id=target(off),
            device_id_type=MESH,
        )
        copy.start()
        return copy


class GatherTp:
    def __init__(self, send, buf, rows, part):
        self.send, self.buf, self.rows, self.part = send, buf, rows, part
        self.core = place()[4]
        self.done = []
        self.sib = []

    def slot(self, k):
        return self.buf.at[self.core, pl.ds(k * self.rows, self.rows)]

    def go(self, src, dst, h, off):
        copy = self.send(self.part(self.slot(src), h), self.part(self.slot(dst), h), off)
        self.done.append(copy)
        return copy

    def sibling(self, k):
        self.sib.append(self.send(self.slot(k), self.slot(k), CORE))

    def p1(self):
        self.z = [self.go(0, 4, 0, ZH), self.go(0, 4, 1, ZH)]
        self.p0 = self.go(0, 1, 0, YP)
        self.m1 = self.go(0, 2, 1, YM)
        self.p1_ = self.go(0, 1, 1, YP)
        self.m0 = self.go(0, 2, 0, YM)
        self.sibling(0)

    def p2(self):
        self.z[0].wait_recv()
        self.q0 = self.go(4, 5, 0, YP)
        self.z[1].wait_recv()
        self.n1 = self.go(4, 6, 1, YM)
        self.q1 = self.go(4, 5, 1, YP)
        self.n0 = self.go(4, 6, 0, YM)
        self.sibling(4)

    def p3(self):
        self.p0.wait_recv()
        self.f1 = self.go(1, 3, 0, YP)
        self.m1.wait_recv()
        self.f2 = self.go(2, 3, 1, YM)
        self.p1_.wait_recv()
        self.sibling(1)
        self.m0.wait_recv()
        self.sibling(2)
        self.q0.wait_recv()
        self.f3 = self.go(5, 7, 0, YP)
        self.n1.wait_recv()
        self.f4 = self.go(6, 7, 1, YM)

    def p4(self):
        self.f1.wait_recv()
        self.f2.wait_recv()
        self.sibling(3)
        self.q1.wait_recv()
        self.sibling(5)
        self.n0.wait_recv()
        self.sibling(6)
        self.f3.wait_recv()
        self.f4.wait_recv()
        self.sibling(7)

    def p5(self):
        for copy in self.sib:
            copy.wait_recv()
        for copy in self.sib + self.done:
            copy.wait_send()

    def all(self):
        self.p1()
        self.p2()
        self.p3()
        self.p4()
        self.p5()


class GatherRep:
    def __init__(self, send, ref, late_z):
        self.send, self.ref, self.late_z = send, ref, late_z
        self.first, self.second, self.third = {}, {}, {}

    def go(self, src, dst, j, off):
        return [self.send(a, b, off) for a, b in zip(self.ref(src, j), self.ref(dst, j, off))]

    def a(self, j):
        self.first[j] = (self.go(0, 4, j, ZL), self.go(0, 1, j, XP), self.go(0, 2, j, XM))

    def b(self, j):
        for copies in self.first[j]:
            for copy in copies:
                copy.wait_recv()
        f = self.go(1, 3, j, XP) if j % 2 == 0 else self.go(2, 3, j, XM)
        if j not in self.late_z:
            more = (self.go(4, 5, j, XP), self.go(4, 6, j, XM))
        else:
            more = (self.go(1, 5, j, ZL), self.go(2, 6, j, ZL))
        self.second[j] = (f,) + more

    def c(self, j):
        for copies in self.second[j]:
            for copy in copies:
                copy.wait_recv()
        if j not in self.late_z:
            self.third[j] = self.go(5, 7, j, XP) if j % 2 == 1 else self.go(6, 7, j, XM)
        else:
            self.third[j] = self.go(3, 7, j, ZL)

    def end(self, j):
        for copy in self.third[j]:
            copy.wait_recv()
        for copies in self.first[j] + self.second[j] + (self.third[j],):
            for copy in copies:
                copy.wait_send()


def columns_part(ref, h):
    return ref.at[:, pl.ds(h * (HALF // 2), HALF // 2)]


def rows_part(ref, h):
    return ref.at[pl.ds(h * (ROWS // 2), ROWS // 2)]


def body(
    scale_up,
    scale_down,
    pick,
    pool_tokens,
    pool_targets,
    up_hbm,
    down_hbm,
    out,
    up,
    down,
    down_own,
    local,
    tok0,
    tok1,
    pre,
    hid,
    ht0,
    ht1,
    sib_send,
    sib_recv,
    part,
    r_far,
    r_near,
    r_z,
    err0,
    es0,
    es1,
    acc,
    grad0,
    base,
    send_sems,
    recv_sems,
    copy_sems,
):
    _, _, _, _, core = place()
    me = lax.axis_index("rep")
    send = Sends(send_sems, recv_sems)

    loads = [
        pltpu.make_async_copy(up_hbm, up, copy_sems.at[0]),
        pltpu.make_async_copy(down_hbm, down, copy_sems.at[1]),
    ]
    for h in range(2):
        cols = pl.ds(pl.multiple_of(h * HALF + me * SLICE, SLICE), SLICE)
        loads.append(pltpu.make_async_copy(down_hbm.at[:, cols], down_own.at[h], copy_sems.at[2 + h]))
    for load in loads:
        load.start()

    peers = (CORE, YP, YM, ZH) + REP[1:]
    barrier = pltpu.get_barrier_semaphore()
    for off in peers:
        pl.semaphore_signal(barrier, inc=1, device_id=target(off), device_id_type=MESH)

    def picked(step, pool, cols):
        row = lax.broadcasted_iota(jnp.int32, (24, 64), 0)
        col = lax.broadcasted_iota(jnp.int32, (24, 64), 1)
        chosen = jnp.zeros((24, 64), jnp.int32)
        for i in range(24):
            chosen = jnp.where(row == i, pick[step, i], chosen)
        return jnp.dot((chosen == col).astype(F32).astype(BF), pool[:, cols], preferred_element_type=F32)

    sources = [(step, pool) for step in range(2) for pool in (pool_tokens, pool_targets)]

    @pl.loop(0, HALF // 512)
    def _(k):
        inner = pl.ds(pl.multiple_of(k % 2 * 512, 512), 512)
        cols = pl.ds(pl.multiple_of((1 - core) * HALF + k * 512, 512), 512)
        part[k // 2, pl.ds(0, 96), inner] = jnp.concatenate([picked(*source, cols) for source in sources], axis=0).astype(BF)

    pl.semaphore_wait(barrier, len(peers))

    prep = send(part.at[:, pl.ds(0, 96)], sib_recv.at[:, pl.ds(0, 96)], CORE)
    prep.wait_recv()

    def assemble(which):
        @pl.loop(0, HALF // 512)
        def _(k):
            inner = pl.ds(pl.multiple_of(k * 512, 512), 512)
            cols = pl.ds(pl.multiple_of(core * HALF + k * 512, 512), 512)
            theirs = sib_recv[k // 2, pl.ds(0, 96), pl.ds(pl.multiple_of(k % 2 * 512, 512), 512)].astype(F32)
            for i in which:
                a, b = picked(*sources[i], cols), theirs[24 * i : 24 * i + 24]
                first, second = jnp.where(core == 0, a, b), jnp.where(core == 0, b, a)
                local[i, :, inner] = jnp.concatenate([first, second], axis=0).astype(BF)

    assemble((0,))
    prep.wait_send()
    tok0[core, pl.ds(0, TOK), :] = local[0]

    def preact(tokens):
        pre[...] = jnp.zeros_like(pre)
        for h in range(2):

            @pl.loop(0, HALF // 1024, unroll=2)
            def _(k):
                cols = pl.ds(pl.multiple_of(k * 1024, 1024), 1024)
                rows = pl.ds(pl.multiple_of(h * HALF + k * 1024, 1024), 1024)
                pre[...] += jnp.dot(tokens[h, :, cols], up[rows, :], preferred_element_type=F32)

    def activate(ht):
        @pl.loop(0, 7)
        def _(k):
            cols = pl.ds(pl.multiple_of(k * 128, 128), 128)
            v = pre[:, cols] * scale_up
            hidden = (v * jax.nn.sigmoid(v)).astype(BF)
            hid[:, cols] = hidden
            ht[0, cols, :] = hidden.T

    def layer_out(base, width, store):
        @pl.loop(0, width // 512, unroll=2)
        def _(k):
            inner = pl.multiple_of(k * 512, 512)
            cols = pl.ds(pl.multiple_of(base + inner, 512), 512)
            store(inner, jnp.dot(hid[...], down[:, cols], preferred_element_type=F32))

    def forward_down(between):
        sib = []
        for h in range(2):

            def to_sibling(inner, value, h=h):
                sib_send[h, :, pl.ds(inner, 512)] = value.astype(BF)

            layer_out((1 - core) * HALF + h * 1024, 1024, to_sibling)
            sib.append(send(sib_send.at[h], sib_recv.at[h], CORE))
        between()
        for h in range(2):
            sib[h].wait_recv()

            def to_part(inner, value, h=h):
                total = value + sib_recv[h, :, pl.ds(inner, 512)].astype(F32)
                part[h, :, pl.ds(inner, 512)] = total.astype(BF)

            layer_out(core * HALF + h * 1024, 1024, to_part)
        for copy in sib:
            copy.wait_send()

    def scatter(hooks=(None, None, None)):
        sent = []

        def go(src, dst, off):
            copy = send(src, dst, off)
            sent.append(copy)
            return copy

        def block(k, h):
            return part.at[h, pl.ds(k * TOK, TOK)]

        far, near = {}, {}
        for p in (1, 0):
            far[p, 0] = go(block(4 * p + 3, 0), r_far.at[p, 0], YP)
            far[p, 1] = go(block(4 * p + 3, 1), r_far.at[p, 1], YM)
            near[p, 0, 1] = go(block(4 * p + 2, 1), r_near.at[p, 0, 1], YP)
            near[p, 1, 0] = go(block(4 * p + 1, 0), r_near.at[p, 1, 0], YM)
        run(hooks[0])
        for p in (1, 0):
            for d, off in ((0, YP), (1, YM)):
                far[p, d].wait_recv()
                rows = pl.ds((4 * p + 2 - d) * TOK, TOK)
                total = part[d, rows, :].astype(F32) + r_far[p, d].astype(F32)
                part[d, rows, :] = total.astype(BF)
                near[p, d, d] = go(block(4 * p + 2 - d, d), r_near.at[p, d, d], off)
        run(hooks[1])
        z = []
        for h in range(2):
            near[1, 0, h].wait_recv()
            near[1, 1, h].wait_recv()
            rows = pl.ds(4 * TOK, TOK)
            total = part[h, rows, :].astype(F32) + r_near[1, 0, h].astype(F32) + r_near[1, 1, h].astype(F32)
            part[h, rows, :] = total.astype(BF)
            z.append(go(block(4, h), r_z.at[h], ZH))
        run(hooks[2])
        halves = []
        for h in range(2):
            near[0, 0, h].wait_recv()
            near[0, 1, h].wait_recv()
            total = part[h, pl.ds(0, TOK), :].astype(F32) + r_near[0, 0, h].astype(F32) + r_near[0, 1, h].astype(F32)
            z[h].wait_recv()
            halves.append(total + r_z[h].astype(F32))
        for copy in sent:
            copy.wait_send()
        return halves

    def error(step, halves, dst, es):
        for h in range(2):
            cols = pl.ds(h * 1024, 1024)
            value = local[2 * step, :, cols].astype(F32) + scale_down * halves[h] - local[2 * step + 1, :, cols].astype(F32)
            dst[:, cols] = value.astype(BF)
        sent = []
        for k in range(1, 8):
            cols = pl.ds(pl.multiple_of(rep_index(REP[k]) * SLICE, SLICE), SLICE)
            sent.append(send(dst.at[:, cols], es.at[core, pl.ds(k * TOK, TOK)], REP[k]))
        cols = pl.ds(pl.multiple_of(me * SLICE, SLICE), SLICE)
        es[core, pl.ds(0, TOK), :] = dst[:, cols]
        return sent

    def hidden_gather(ht):
        size = ht.shape[1] // CHUNKS
        return GatherRep(send, lambda slot, j, off=None: [ht.at[slot, pl.ds(j * size, size)]], (3,))

    gather = GatherTp(send, tok0, TOK, columns_part)
    gather.p1()
    assemble((1, 2, 3))
    tok1[core, pl.ds(0, TOK), :] = local[2]
    gather.p2()
    gather.p3()
    gather.p4()
    gather.p5()
    late = GatherTp(send, tok1, TOK, columns_part)
    late.p1()
    loads[0].wait()
    preact(tok0)
    late.p2()
    activate(ht0)
    rep0 = hidden_gather(ht0)
    for j in range(CHUNKS):
        rep0.a(j)
    loads[1].wait()
    forward_down(late.p3)
    halves = scatter()
    late.p4()
    sliced = error(0, halves, err0.at[core, pl.ds(0, TOK)], es0)
    def transpose_tokens(quarter):
        h = quarter // 2

        @pl.loop(0, 4)
        def _(k):
            inner = pl.multiple_of(quarter % 2 * 1024 + k * 256, 256)
            wide = pl.multiple_of(h * HALF + inner, 256)
            turned = tok0[h, :, pl.ds(inner, 256)].T
            grad0[pl.ds(wide, 256), :] = turned[:, :256]
            grad0[pl.ds(2 * HALF + wide, 256), pl.ds(0, 128)] = turned[:, 256:]

    gather = GatherTp(send, err0, TOK, columns_part)
    gather.p1()
    transpose_tokens(0)
    for j in range(CHUNKS):
        rep0.b(j)
    gather.p2()
    transpose_tokens(1)
    gather.p3()
    transpose_tokens(2)
    gather.p4()
    transpose_tokens(3)
    gather.p5()
    for copy in sliced:
        copy.wait()
    slices = GatherTp(send, es0, ROWS, rows_part)
    slices.p1()

    acc[...] = jnp.zeros_like(acc)
    for h in range(2):

        @pl.loop(0, HALF // 1024, unroll=2)
        def _(k):
            cols = pl.ds(pl.multiple_of(k * 1024, 1024), 1024)
            wide = pl.ds(pl.multiple_of(h * HALF + k * 1024, 1024), 1024)
            acc[...] += lax.dot_general(
                err0[h, :, cols], down[:, wide], (((1,), (1,)), ((), ())), preferred_element_type=F32
            )

    @pl.loop(0, 3)
    def _(n):
        rows = pl.ds(pl.multiple_of(n * 128, 128), 128)
        v = pre[rows, :] * scale_up
        sigma = jax.nn.sigmoid(v)
        hid[rows, :] = (scale_down * acc[rows, :] * (sigma * (1.0 + v * (1.0 - sigma)))).astype(BF)

    slices.p2()
    for h in range(2):

        @pl.loop(0, HALF // 256, unroll=2)
        def _(k):
            wide = pl.multiple_of(h * HALF + k * 256, 256)
            rows = pl.ds(wide, 256)
            g = jnp.dot(grad0[rows, :], hid[pl.ds(0, 256), :], preferred_element_type=F32)
            g += jnp.dot(
                grad0[pl.ds(2 * HALF + wide, 256), pl.ds(0, 128)], hid[pl.ds(256, 128), :], preferred_element_type=F32
            )
            u = g * inverse(jnp.abs(g) + 0.02 / scale_up)
            up[rows, :] = (0.975 * up[rows, :].astype(F32) - 0.25 * u).astype(BF)

    slices.p3()
    for j in range(CHUNKS):
        rep0.c(j)
    late.p5()

    preact(tok1)
    activate(ht1)
    rep1 = hidden_gather(ht1)
    for j in range(CHUNKS):
        rep1.a(j)
    for h in range(2):

        @pl.loop(0, HALF // 256, unroll=2)
        def _(k):
            cols = pl.ds(pl.multiple_of(k * 256, 256), 256)
            wide = pl.ds(pl.multiple_of(h * HALF + k * 256, 256), 256)
            g = jnp.dot(ht0[0], err0[h, :, cols], preferred_element_type=F32)
            u = g * inverse(jnp.abs(g) + 0.02 / scale_down)
            down[:, wide] = (0.975 * down[:, wide].astype(F32) - 0.25 * u).astype(BF)

    slices.p4()
    for j in range(CHUNKS):
        rep0.end(j)

    es0_view = es0.reshape(2, 8, ROWS, SLICE)
    es1_view = es1.reshape(2, 8, ROWS, SLICE)
    size = 896 // CHUNKS

    def slice_of(view, h, k):
        tokens = pl.ds(k * TOK if isinstance(k, int) else pl.multiple_of(k * TOK, TOK), TOK)
        return view[h, :, tokens, :].reshape(ROWS, SLICE)

    def first_update(k):
        for h in range(2):
            e = slice_of(es0_view, h, k)

            @pl.loop(0, CHUNKS)
            def _(j):
                rows = pl.ds(pl.multiple_of(j * size, size), size)
                kept = pl.ds(pl.multiple_of((k * 2 + h) * 896 + j * size, 32), size)
                g = jnp.dot(ht0[k, rows, :], e, preferred_element_type=F32)
                u = g * inverse(jnp.abs(g) + 0.02 / scale_down)
                grad0[kept, :] = g.astype(BF)
                if k == 0:
                    base[h, rows, :] = 0.975 * u
                else:
                    base[h, rows, :] += 0.975 * u

    def both(k, then=None):
        def hook():
            first_update(k)
            run(then)

        return hook

    forward_down(slices.p5)
    rep1.b(0)
    halves = scatter((both(0, lambda: rep1.b(1)), both(1, lambda: rep1.b(2)), both(2, lambda: rep1.b(3))))
    sliced = error(1, halves, local.at[0], es1)
    rep1.c(0)
    first_update(3)
    for copy in sliced:
        copy.wait()
    last = GatherTp(send, es1, ROWS, rows_part)
    last.p1()
    rep1.c(1)
    first_update(4)
    last.p2()
    rep1.c(2)
    first_update(5)
    last.p3()
    rep1.c(3)
    first_update(6)
    last.p4()
    first_update(7)
    last.p5()
    for j in range(CHUNKS):
        rep1.end(j)
    loads[2].wait()
    loads[3].wait()

    def reduce(j, h):
        rows = pl.ds(j * size, size)

        def one(k, total):
            g0 = grad0[pl.ds(pl.multiple_of((k * 2 + h) * 896 + j * size, 32), size), :].astype(F32)
            g1 = jnp.dot(ht1[k, rows, :], slice_of(es1_view, h, k), preferred_element_type=F32)
            first = (0.09 / 0.19) * g0 + (0.1 / 0.19) * g1
            second = (0.0475 / 0.0975) * (g0 * g0) + (0.05 / 0.0975) * (g1 * g1)
            root = second * lax.rsqrt(jnp.maximum(second, 1e-30))
            return total + first * inverse(root + 0.02 / scale_down)

        total = lax.fori_loop(0, 8, one, base[h, rows, :], unroll=2)
        w = down_own[h, rows, :].astype(F32)
        average = (1.0 - 0.975 * 0.975) * w + (0.25 / 8.0) * total
        down_own[h, rows, :] = (w - 0.7 * 1.9 * average).astype(BF)

    def pieces(slot, n, off=None):
        h, rows = n // CHUNKS, pl.ds(n % CHUNKS * size, size)
        if slot == 0:
            return [down_own.at[h, rows]]
        back = REP[slot]
        shift = off if off is not None else (0, 0)
        r = rep_index((shift[0] - back[0] + 4, shift[1] - back[1] + 2))
        return [out.at[rows, pl.ds(pl.multiple_of(h * HALF + r * SLICE, SLICE), SLICE)]]

    final = GatherRep(send, pieces, (0, 3, 6))
    own = []
    total = 2 * CHUNKS
    for n in range(total + LAG_C):
        if n < total:
            h, j = n // CHUNKS, n % CHUNKS
            reduce(j, h)
            final.a(n)
            cols = pl.ds(pl.multiple_of(h * HALF + me * SLICE, SLICE), SLICE)
            rows = pl.ds(j * size, size)
            own.append(pltpu.make_async_copy(down_own.at[h, rows], out.at[rows, cols], copy_sems.at[4 + n]))
            own[-1].start()
        if 0 <= n - LAG_B < total:
            final.b(n - LAG_B)
        if 0 <= n - LAG_C < total:
            final.c(n - LAG_C)
    for n in range(total):
        final.end(n)
    for copy in own:
        copy.wait()


LAG_B, LAG_C = 2, 3
SEMS = 300


def round_kernel(pick, pool_tokens, pool_targets, up_weight, down_weight, scale_up, scale_down):
    vmem, anywhere = pl.BlockSpec(memory_space=pltpu.VMEM), pl.BlockSpec(memory_space=pl.ANY)
    width, hidden = up_weight.shape
    return pl.pallas_call(
        functools.partial(body, scale_up, scale_down),
        out_shape=jax.ShapeDtypeStruct(down_weight.shape, BF),
        in_specs=[pl.BlockSpec(memory_space=pltpu.SMEM), vmem, vmem, anywhere, anywhere],
        out_specs=anywhere,
        scratch_shapes=[
            pltpu.VMEM((width, hidden), BF),
            pltpu.VMEM((hidden, width), BF),
            pltpu.VMEM((2, hidden, SLICE), BF),
            pltpu.VMEM((4, TOK, HALF), BF),
            pltpu.VMEM((2, ROWS, HALF), BF),
            pltpu.VMEM((2, ROWS, HALF), BF),
            pltpu.VMEM((ROWS, hidden), F32),
            pltpu.VMEM((ROWS, hidden), BF),
            pltpu.VMEM((8, hidden, ROWS), BF),
            pltpu.VMEM((8, hidden, ROWS), BF),
            pltpu.VMEM((2, ROWS, HALF // 2), BF),
            pltpu.VMEM((2, ROWS, HALF // 2), BF),
            pltpu.VMEM((2, ROWS, HALF // 2), BF),
            pltpu.VMEM((2, 2, TOK, HALF // 2), BF),
            pltpu.VMEM((2, 2, 2, TOK, HALF // 2), BF),
            pltpu.VMEM((2, TOK, HALF // 2), BF),
            pltpu.VMEM((2, ROWS, HALF), BF),
            pltpu.VMEM((2, 8 * ROWS, SLICE), BF),
            pltpu.VMEM((2, 8 * ROWS, SLICE), BF),
            pltpu.VMEM((ROWS, hidden), F32),
            pltpu.VMEM((16 * hidden, SLICE), BF),
            pltpu.VMEM((2, hidden, SLICE), F32),
            pltpu.SemaphoreType.DMA((SEMS,)),
            pltpu.SemaphoreType.DMA((SEMS,)),
            pltpu.SemaphoreType.DMA((4 + 2 * CHUNKS,)),
        ],
        compiler_params=pltpu.CompilerParams(
            collective_id=0, has_side_effects=True, vmem_limit_bytes=63 * 2**20
        ),
    )(pick, pool_tokens, pool_targets, up_weight, down_weight)


def per_device(pool_tokens, pool_targets, pick, up_weight, down_weight):
    scale_up = 1.0 / math.sqrt(up_weight.shape[0])
    scale_down = 1.0 / math.sqrt(up_weight.shape[1] * lax.axis_size("tp"))
    return round_kernel(pick[0], pool_tokens, pool_targets, up_weight, down_weight, scale_up, scale_down)


def solution(mesh):
    in_specs = (P("tp", None), P("tp", None), P("rep", None, "tp"), P(None, "tp"), P("tp", None))
    return jax.shard_map(per_device, mesh=mesh, in_specs=in_specs, out_specs=P("tp", None), check_vma=False)
```
